128 devices in a mesh: dp: 2 (over x_lo), expert: 64 (over z, x_hi, y, core).
Axes of the slice: x: 4 (x_hi: 2, x_lo: 2; x = x_hi * 2 + x_lo), y: 4, z: 4, core: 2. Of those that a mesh axis runs over, the one named last changes fastest.
Arguments:
- tokens: bfloat16 [32768, 1024], P(('dp', 'expert')), may hold values from -6 to 6
- modulation: bfloat16 [128, 2, 1024], P(('dp', 'expert')), may hold values from -3 to 3
- router_weight: bfloat16 [1024, 64], replicated, may hold values from -0.1875 to 0.1875
- weight_in: bfloat16 [64, 1024, 4096], P('expert', None, 'dp'), may hold values from -0.1875 to 0.1875
- weight_out: bfloat16 [64, 4096, 1024], P('expert', 'dp'), may hold values from -0.09375 to 0.09375
- chosen: int32 [2, 64, 256], P('dp'), may hold values from 0 to 16383, as said below
- grad_out: bfloat16 [32768, 1024], P(('dp', 'expert')), may hold values from -4 to 4
Outputs:
- grad_tokens: bfloat16 [32768, 1024], P(('dp', 'expert'))
- grad_mod: float32 [128, 2, 1024], P(('dp', 'expert'))
- grad_router: float32 [1024, 64], replicated
- grad_weight_in: bfloat16 [64, 1024, 4096], P('expert', None, 'dp')
- grad_weight_out: bfloat16 [64, 4096, 1024], P('expert', 'dp')
The draws below stay inside these ranges and needn't reach their ends.
Inputs may be any that keep to these rules, and one draw needn't show every extreme that they name: `chosen`: for each slice and expert the 256 positions are distinct; at most 8 of them lie in one image's 256 tokens, and in one image exactly 8.
All inputs are finite; a program needn't handle non-finite values.
Results may differ from the reference program's by a relative error of at most 0.008.
Values may be sent and summed in bfloat16 or wider, within the bound.
A program may use at most 128 MiB of HBM per device.

```python
import jax
import jax.numpy as jnp
from jax import lax

D = 1024
HID = 4096
TOK_DEV = 256
EXPERTS = 64
IMAGES = 128
TOKENS = 32768
SLICE = 16384
CAP = 256
MOST = 8
N_DP = 2


def draw_chosen(key, part):
    slices = IMAGES // EXPERTS
    images = SLICE // TOK_DEV
    pairs = images // 2

    def one_list(list_key):
        order_key, split_key, rows_key = jax.random.split(list_key, 3)
        order = jax.random.permutation(order_key, images)
        splits = jax.random.randint(split_key, (pairs,), 0, MOST + 1)
        splits = splits.at[0].set(MOST)
        pair_counts = jnp.stack([splits, MOST - splits], axis=1).reshape(-1)
        counts = jnp.zeros((images,), jnp.int32).at[order].set(pair_counts.astype(jnp.int32))
        row_keys = jax.random.split(rows_key, images)
        picked = jax.vmap(lambda each_key: jax.random.permutation(each_key, TOK_DEV)[:MOST])(row_keys)
        slot_index = jnp.arange(MOST, dtype=jnp.int32)[None, :]
        is_valid = slot_index < counts[:, None]
        global_rows = jnp.arange(images, dtype=jnp.int32)[:, None] * TOK_DEV + picked.astype(jnp.int32)
        ranking = jnp.where(is_valid, 0, 1) * (images * MOST) + jnp.arange(images * MOST, dtype=jnp.int32).reshape(images, MOST)
        keep = jnp.argsort(ranking.reshape(-1), stable=True)[:CAP]
        return global_rows.reshape(-1)[keep].astype(jnp.int32)
    list_keys = jax.random.split(jax.random.fold_in(key, 17), slices * EXPERTS)
    return jax.vmap(one_list)(list_keys).reshape(slices, EXPERTS, CAP).astype(jnp.int32)


def block_levels(key, extent, shards, low, largest):
    gain = 1.0
    for dim, shards_of in shards:
        draws = jax.random.uniform(jax.random.fold_in(jax.random.fold_in(key, 6), dim), (shards_of,), jnp.float32, low / len(shards), largest / len(shards))
        gain = gain * jnp.repeat(jnp.exp(draws), extent[dim] // shards_of).reshape((-1,) + (1,) * (len(extent) - 1 - dim))
    return gain


def noise(rng, shape, scale, most, cuts=(), kind=jnp.bfloat16):
    level = block_levels(rng, shape, cuts, -0.22, 0.18) if cuts else 1.0
    array = jax.random.normal(rng, shape, jnp.float32) * scale * level
    return jnp.minimum(jnp.maximum(array, -most), most).astype(kind)


def setup_inputs(seed: int = 0) -> dict:
    arg_keys = jax.random.split(jax.random.key(seed), 8)
    return {
        "tokens": noise(arg_keys[0], (TOKENS, D), 1.0, 6.0, ((0, 128),)),
        "modulation": noise(arg_keys[1], (IMAGES, 2, D), 0.5, 3.0, ((0, 128),)),
        "router_weight": noise(arg_keys[2], (D, EXPERTS), D ** -0.5, 0.1875),
        "weight_in": noise(arg_keys[3], (EXPERTS, D, HID), D ** -0.5, 0.1875, ((0, 64), (2, 2))),
        "weight_out": noise(arg_keys[4], (EXPERTS, HID, D), HID ** -0.5, 0.09375, ((0, 64), (1, 2))),
        "chosen": draw_chosen(jax.random.fold_in(arg_keys[7], 71), 0),
        "grad_out": noise(arg_keys[6], (TOKENS, D), 0.5, 4.0, ((0, 128),)),
    }


gelu_root = 0.7978845608028654
gelu_cube = 0.044715
norm_eps = 1e-06

def gelu_value(values):
    inner = gelu_root * (values + gelu_cube * values * values * values)
    return 0.5 * values * (1.0 + jnp.tanh(inner))

def gelu_slope(values):
    tangent = jnp.tanh(gelu_root * (values + gelu_cube * values * values * values))
    return 0.5 * (1.0 + tangent) + 0.5 * values * (1.0 - tangent * tangent) * gelu_root * (1.0 + 3.0 * gelu_cube * values * values)

def expert_terms(rows_u, rows_g, rows_p, first_w, second_w):
    preact = jnp.dot(rows_u, first_w, preferred_element_type=jnp.float32)
    hidden = gelu_value(preact).astype(jnp.bfloat16)
    upstream = lax.dot_general(rows_g, second_w, (((1,), (1,)), ((), ())), preferred_element_type=jnp.float32)
    score_sum = lax.optimization_barrier(jnp.sum(hidden.astype(jnp.float32) * upstream, axis=1))
    prob_col = rows_p.astype(jnp.float32)[:, None]
    grad_y = (prob_col * rows_g.astype(jnp.float32)).astype(jnp.bfloat16)
    grad_pre = (prob_col * upstream * gelu_slope(preact)).astype(jnp.bfloat16)
    return (hidden, score_sum, grad_y, grad_pre)

def reference(tokens, modulation, router_weight, weight_in, weight_out, chosen, grad_out):
    x_float = tokens.astype(jnp.float32)
    average = lax.optimization_barrier(jnp.mean(x_float, axis=1, keepdims=True))
    centred = x_float - average
    spread = lax.optimization_barrier(jnp.mean(centred * centred, axis=1, keepdims=True))
    inverse = lax.rsqrt(spread + norm_eps)
    normed = centred * inverse
    mod_float = modulation.astype(jnp.float32)
    shift_rows = jnp.repeat(mod_float[:, 0], TOK_DEV, axis=0)
    scale_rows = jnp.repeat(mod_float[:, 1], TOK_DEV, axis=0)
    normal_u = (normed * (1.0 + scale_rows) + shift_rows).astype(jnp.bfloat16)
    gate_prob = jax.nn.sigmoid(jnp.dot(normal_u, router_weight, preferred_element_type=jnp.float32)).astype(jnp.bfloat16)
    slice_start = jnp.arange(N_DP, dtype=jnp.int32) * SLICE
    global_ids = chosen + slice_start[:, None, None]
    per_expert = jnp.transpose(global_ids, (1, 0, 2)).reshape(EXPERTS, N_DP * CAP).astype(jnp.int32)
    expert_index = jnp.arange(EXPERTS, dtype=jnp.int32)

    def one_expert(packed):
        first_w, second_w, row_ids, index = packed
        rows_u = normal_u[row_ids]
        rows_g = grad_out[row_ids]
        rows_p = gate_prob[row_ids, index]
        hidden, score_sum, grad_y, grad_pre = expert_terms(rows_u, rows_g, rows_p, first_w, second_w)
        grad_first = lax.dot_general(rows_u, grad_pre, (((0,), (0,)), ((), ())), preferred_element_type=jnp.float32).astype(jnp.bfloat16)
        grad_second = lax.dot_general(hidden, grad_y, (((0,), (0,)), ((), ())), preferred_element_type=jnp.float32).astype(jnp.bfloat16)
        grad_rows = lax.dot_general(grad_pre, first_w, (((1,), (1,)), ((), ())), preferred_element_type=jnp.float32).astype(jnp.bfloat16)
        return (grad_first, grad_second, grad_rows, score_sum.astype(jnp.bfloat16))
    grads_first, grads_second, grad_rows, scores = lax.map(one_expert, (weight_in, weight_out, per_expert, expert_index))
    flat_ids = per_expert.reshape(-1)
    flat_experts = jnp.repeat(expert_index, N_DP * CAP)
    grad_u = jnp.zeros((TOKENS, D), jnp.float32).at[flat_ids].add(grad_rows.reshape(-1, D).astype(jnp.float32))
    prob_sel = gate_prob[flat_ids, flat_experts].astype(jnp.float32)
    logit_terms = scores.reshape(-1).astype(jnp.float32) * prob_sel * (1.0 - prob_sel)
    grad_logit = jnp.zeros((TOKENS, EXPERTS), jnp.float32).at[flat_ids, flat_experts].add(logit_terms)
    grad_u = grad_u + jnp.dot(grad_logit, router_weight.astype(jnp.float32).T, precision=lax.Precision.HIGHEST)
    grad_router = jnp.dot(normal_u.astype(jnp.float32).T, grad_logit, precision=lax.Precision.HIGHEST)
    grad_image = grad_u.reshape(IMAGES, TOK_DEV, D)
    grad_shift = lax.optimization_barrier(jnp.sum(grad_image, axis=1))
    grad_scale = lax.optimization_barrier(jnp.sum(grad_image * normed.reshape(IMAGES, TOK_DEV, D), axis=1))
    grad_mod = jnp.stack([grad_shift, grad_scale], axis=1)
    grad_norm = grad_u * (1.0 + scale_rows)
    centre_term = lax.optimization_barrier(jnp.mean(grad_norm, axis=1, keepdims=True))
    slope_term = lax.optimization_barrier(jnp.mean(grad_norm * normed, axis=1, keepdims=True))
    grad_tokens = (grad_out.astype(jnp.float32) + (grad_norm - centre_term - normed * slope_term) * inverse).astype(jnp.bfloat16)
    return (grad_tokens, grad_mod, grad_router, grads_first, grads_second)
```

```python
import jax
import jax.numpy as jnp
from jax import lax
from jax.sharding import PartitionSpec as P

gelu_root = 0.7978845608028654
gelu_cube = 0.044715
norm_eps = 1e-06


def gelu_value(values):
    inner = gelu_root * (values + gelu_cube * values * values * values)
    return 0.5 * values * (1.0 + jnp.tanh(inner))


def gelu_slope(values):
    tangent = jnp.tanh(gelu_root * (values + gelu_cube * values * values * values))
    return 0.5 * (1.0 + tangent) + 0.5 * values * (1.0 - tangent * tangent) * gelu_root * (
        1.0 + 3.0 * gelu_cube * values * values
    )


def finish_terms(preact, upstream, rows_g, rows_p):
    hidden = gelu_value(preact).astype(jnp.bfloat16)
    score_sum = jnp.sum(hidden.astype(jnp.float32) * upstream, axis=1)
    prob_col = rows_p.astype(jnp.float32)[:, None]
    grad_y = (prob_col * rows_g.astype(jnp.float32)).astype(jnp.bfloat16)
    grad_pre = (prob_col * upstream * gelu_slope(preact)).astype(jnp.bfloat16)
    return (hidden, score_sum, grad_y, grad_pre)


def body(tokens, modulation, router_weight, weight_in, weight_out, chosen, grad_out):
    tok_count = tokens.shape[0]
    model_width = tokens.shape[1]
    experts = lax.axis_size("expert")
    my_index = lax.axis_index("expert")
    most_rows = 2 * tok_count // experts
    x_float = tokens.astype(jnp.float32)
    average = jnp.mean(x_float, axis=1, keepdims=True)
    centred = x_float - average
    spread = jnp.mean(centred * centred, axis=1, keepdims=True)
    inverse = lax.rsqrt(spread + norm_eps)
    normed = centred * inverse
    shift_mod = modulation[0, 0].astype(jnp.float32)
    scale_mod = modulation[0, 1].astype(jnp.float32)
    normal_u = (normed * (1.0 + scale_mod) + shift_mod).astype(jnp.bfloat16)
    gate_prob = jax.nn.sigmoid(
        jnp.dot(normal_u, router_weight, preferred_element_type=jnp.float32)
    ).astype(jnp.bfloat16)
    picked = chosen[0]
    local_row = picked - my_index * tok_count
    is_mine = (local_row >= 0) & (local_row < tok_count)
    list_len = picked.shape[1]
    list_pos = jnp.arange(list_len, dtype=jnp.int32)
    before = (list_pos[:, None] < list_pos[None, :]).astype(jnp.bfloat16)
    rank_in = jnp.dot(
        is_mine.astype(jnp.bfloat16), before, preferred_element_type=jnp.float32
    ).astype(jnp.int32)
    slot_at = jnp.where(is_mine, rank_in, most_rows)
    expert_col = jnp.arange(experts, dtype=jnp.int32)[:, None]
    rows_idx = (
        jnp.full((experts, most_rows), tok_count, jnp.int32)
        .at[expert_col, slot_at]
        .set(local_row, mode="drop")
    )
    u_pad = jnp.concatenate([normal_u, jnp.zeros((1, model_width), jnp.bfloat16)], axis=0)
    g_pad = jnp.concatenate([grad_out, jnp.zeros((1, model_width), jnp.bfloat16)], axis=0)
    p_pad = jnp.concatenate([gate_prob, jnp.zeros((1, experts), jnp.bfloat16)], axis=0)
    u_send = u_pad[rows_idx]
    g_send = g_pad[rows_idx]
    p_send = p_pad[rows_idx, expert_col]
    u_recv, g_recv, p_recv = (
        lax.all_to_all(u_send, "expert", split_axis=0, concat_axis=0, tiled=True),
        lax.all_to_all(g_send, "expert", split_axis=0, concat_axis=0, tiled=True),
        lax.all_to_all(p_send, "expert", split_axis=0, concat_axis=0, tiled=True),
    )
    u_all, g_all, p_all = (
        lax.all_gather(u_recv, "dp", axis=0, tiled=True),
        lax.all_gather(g_recv, "dp", axis=0, tiled=True),
        lax.all_gather(p_recv, "dp", axis=0, tiled=True),
    )
    rows_u = u_all.reshape(-1, model_width)
    rows_g = g_all.reshape(-1, model_width)
    rows_p = p_all.reshape(-1)
    first_w = weight_in[0]
    second_w = weight_out[0]
    preact = jnp.dot(rows_u, first_w, preferred_element_type=jnp.float32)
    upstream = lax.dot_general(
        rows_g, second_w, (((1,), (1,)), ((), ())), preferred_element_type=jnp.float32
    )
    hidden, score_sum, grad_y, grad_pre = finish_terms(preact, upstream, rows_g, rows_p)
    grad_first = lax.dot_general(
        rows_u, grad_pre, (((0,), (0,)), ((), ())), preferred_element_type=jnp.float32
    )
    grad_second = lax.dot_general(
        hidden, grad_y, (((0,), (0,)), ((), ())), preferred_element_type=jnp.float32
    )
    rows_part = lax.dot_general(
        grad_pre, first_w, (((1,), (1,)), ((), ())), preferred_element_type=jnp.float32
    )
    grad_sum, score_total = (
        lax.psum_scatter(
            rows_part.reshape(-1, most_rows, model_width), "dp", scatter_dimension=0, tiled=True
        ),
        lax.psum_scatter(score_sum.reshape(-1, most_rows), "dp", scatter_dimension=0, tiled=True),
    )
    grad_weight_in = grad_first.astype(jnp.bfloat16)[None]
    grad_weight_out = grad_second.astype(jnp.bfloat16)[None]
    grad_back = grad_sum.astype(jnp.bfloat16)
    score_back = score_total.astype(jnp.bfloat16)
    grad_ret, score_ret = (
        lax.all_to_all(grad_back, "expert", split_axis=0, concat_axis=0, tiled=True),
        lax.all_to_all(score_back, "expert", split_axis=0, concat_axis=0, tiled=True),
    )
    grad_u = (
        jnp.zeros((tok_count + 1, model_width), jnp.float32)
        .at[rows_idx]
        .add(grad_ret.astype(jnp.float32))[:tok_count]
    )
    prob_sent = p_send.astype(jnp.float32)
    logit_terms = score_ret.astype(jnp.float32) * prob_sent * (1.0 - prob_sent)
    grad_logit = (
        jnp.zeros((tok_count + 1, experts), jnp.float32)
        .at[rows_idx, expert_col]
        .add(logit_terms)[:tok_count]
    )
    grad_u = grad_u + jnp.dot(
        grad_logit, router_weight.astype(jnp.float32).T, precision=lax.Precision.HIGHEST
    )
    router_term = jnp.dot(
        normal_u.astype(jnp.float32).T, grad_logit, precision=lax.Precision.HIGHEST
    )
    grad_router = lax.psum(router_term, ("dp", "expert"))
    grad_shift = jnp.sum(grad_u, axis=0)
    grad_scale = jnp.sum(grad_u * normed, axis=0)
    grad_mod = jnp.stack([grad_shift, grad_scale], axis=0)[None]
    grad_norm = grad_u * (1.0 + scale_mod)
    centre_term = jnp.mean(grad_norm, axis=1, keepdims=True)
    slope_term = jnp.mean(grad_norm * normed, axis=1, keepdims=True)
    grad_tokens = (
        grad_out.astype(jnp.float32) + (grad_norm - centre_term - normed * slope_term) * inverse
    ).astype(jnp.bfloat16)
    return (grad_tokens, grad_mod, grad_router, grad_weight_in, grad_weight_out)


def solution(mesh):
    placed = (
        P(("dp", "expert"), None),
        P(("dp", "expert"), None, None),
        P(),
        P("expert", None, "dp"),
        P("expert", "dp", None),
        P("dp", None, None),
        P(("dp", "expert"), None),
    )
    return jax.shard_map(
        body,
        mesh=mesh,
        in_specs=placed,
        out_specs=(
            P(("dp", "expert"), None),
            P(("dp", "expert"), None, None),
            P(),
            P("expert", None, "dp"),
            P("expert", "dp", None),
        ),
        check_vma=False,
    )
```

```python
import jax
import jax.numpy as jnp
from jax import lax
from jax.experimental import pallas as pl
from jax.experimental.pallas import tpu as pltpu
from jax.sharding import PartitionSpec as P

gelu_root = 0.7978845608028654
gelu_cube = 0.044715
norm_eps = 1e-06

TOK = 256
WIDTH = 1024
HALF = 512
HIDL = 2048
EXPERTS = 64
CAP = 256
SLOTS = EXPERTS * 16
TILE = 256
F32 = jnp.float32
BF16 = jnp.bfloat16
MESH = pl.DeviceIdType.MESH


def iota(shape, dim):
    return lax.broadcasted_iota(jnp.int32, shape, dim)


def dot(a, b):
    return jnp.dot(a, b, preferred_element_type=F32)


def dot_nt(a, b):
    return lax.dot_general(a, b, (((1,), (1,)), ((), ())), preferred_element_type=F32)


def dot_tn(a, b):
    return lax.dot_general(a, b, (((0,), (0,)), ((), ())), preferred_element_type=F32)


def kernel(
    tok_ref, mod_ref, rw_ref, w_in_hbm, w_out_hbm, chosen_ref, go_ref,
    gt_ref, gm_ref, gr_ref, gwi_hbm, gwo_hbm,
    w_in, w_out, stage_in, stage_out, sel, comp, comp_t,
    g_send, u_send, g_recv, u_recv, g_all, u_all, gy_all,
    up_scr, hid, gp, own_part, par_send, par_recv, ret_send, ret_recv,
    halves, normed, inverse, scores, q_all, logit, col_mine, col_theirs, col_sum, col_recv, rw_row,
    w_sem, out_sem, send_sem, recv_sem, pair_send, pair_recv,
):
    d = lax.axis_index("dp")
    me = lax.axis_index("expert")
    other = 1 - d

    load_out = pltpu.make_async_copy(w_out_hbm.at[0], w_out, w_sem.at[0])
    load_in = pltpu.make_async_copy(w_in_hbm.at[0], w_in, w_sem.at[1])
    load_out.start()
    load_in.start()

    barrier = pltpu.get_barrier_semaphore()

    def greet(step, carry):
        pl.semaphore_signal(
            barrier, inc=1, device_id=(d, (me + step) & (EXPERTS - 1)), device_id_type=MESH
        )
        return carry

    lax.fori_loop(1, EXPERTS, greet, 0)
    pl.semaphore_signal(barrier, inc=1, device_id=(other, me), device_id_type=MESH)

    local = chosen_ref[0] - me * TOK
    mine = (local >= 0) & (local < TOK)
    before = jnp.where(iota((CAP, CAP), 0) < iota((CAP, CAP), 1), 1.0, 0.0).astype(BF16)
    rank = dot(jnp.where(mine, 1.0, 0.0).astype(BF16), before)
    local_f = (local + 1).astype(F32)
    lane = iota((EXPERTS, 128), 1)
    values = jnp.zeros((EXPERTS, 128), F32)
    for k in range(8):
        one = jnp.sum(
            jnp.where(mine & (rank == float(k)), local_f, 0.0), axis=1, keepdims=True
        )
        values = jnp.where(lane == k, one, values)
    values = values.astype(BF16)

    def fill_sel(i, carry):
        rows = pl.multiple_of(i * TILE, TILE)
        row = rows + iota((TILE, EXPERTS), 0)
        expert = ((row >> 4) + me) & (EXPERTS - 1)
        spread = dot(jnp.where(expert == iota((TILE, EXPERTS), 1), 1.0, 0.0).astype(BF16), values)
        row_k = iota((TILE, 128), 0) & 7
        token = jnp.sum(
            jnp.where(row_k == iota((TILE, 128), 1), spread, 0.0), axis=1, keepdims=True
        )
        part = ((iota((TILE, 1), 0) >> 3) & 1).astype(F32) * float(TOK)
        target = jnp.where(token > 0.5, token - 1.0 + part, -1.0)
        sel[pl.ds(rows, TILE), :] = jnp.where(
            iota((TILE, 2 * TOK), 1).astype(F32) == target, 1.0, 0.0
        ).astype(BF16)
        return carry

    lax.fori_loop(0, SLOTS // TILE, fill_sel, 0)

    def spread_rows(out):
        def step(i, carry):
            rows = pl.multiple_of(i * TILE, TILE)
            out[pl.ds(rows, TILE), :] = dot(sel[pl.ds(rows, TILE), :], halves[...]).astype(BF16)
            return carry

        lax.fori_loop(0, SLOTS // TILE, step, 0)

    def send_all(src, dst, which, sign, size):
        def step(i, carry):
            rows = pl.ds(pl.multiple_of(i * size, size), size)
            pltpu.make_async_remote_copy(
                src_ref=src.at[rows],
                dst_ref=dst.at[rows],
                send_sem=send_sem.at[which],
                recv_sem=recv_sem.at[which],
                device_id=(d, (me + sign * i + EXPERTS) & (EXPERTS - 1)),
                device_id_type=MESH,
            ).start()
            return carry

        lax.fori_loop(1, EXPERTS, step, 0)

    def all_of(src, dst, which, size):
        rows = pl.ds(size, (EXPERTS - 1) * size)
        return pltpu.make_async_remote_copy(
            src_ref=src.at[rows],
            dst_ref=dst.at[rows],
            send_sem=send_sem.at[which],
            recv_sem=recv_sem.at[which],
            device_id=(d, (me + 1) & (EXPERTS - 1)),
            device_id_type=MESH,
        )

    def to_partner(src, dst, which):
        return pltpu.make_async_remote_copy(
            src_ref=src,
            dst_ref=dst,
            send_sem=pair_send.at[which],
            recv_sem=pair_recv.at[which],
            device_id=(other, me),
            device_id_type=MESH,
        )

    halves[0:TOK, :] = go_ref[:, 0:HALF]
    halves[TOK:, :] = go_ref[:, HALF:]
    spread_rows(g_send)
    pl.semaphore_wait(barrier, EXPERTS)
    send_all(g_send, g_recv, 0, 1, 16)
    g_recv[0:16, :] = g_send[0:16, :]

    shift = mod_ref[0, 0:1, :].astype(F32)
    scale = 1.0 + mod_ref[0, 1:2, :].astype(F32)
    x = tok_ref[...].astype(F32)
    centred = x - jnp.mean(x, axis=1, keepdims=True)
    inv = lax.rsqrt(jnp.mean(centred * centred, axis=1, keepdims=True) + norm_eps)
    nrm = centred * inv
    normed[...] = nrm
    inverse[...] = jnp.broadcast_to(inv, (TOK, 128))
    u = (nrm * scale + shift).astype(BF16)
    halves[0:TOK, :] = u[:, 0:HALF]
    halves[TOK:, :] = u[:, HALF:]
    spread_rows(u_send)
    send_all(u_send, u_recv, 1, 1, 16)
    u_recv[0:16, :] = u_send[0:16, :]

    one_row = chosen_ref[0, pl.ds(me, 1), :]
    img_row = one_row >> 8
    r_i, c_i = iota((CAP, CAP), 0), iota((CAP, CAP), 1)
    img_col = jnp.sum(jnp.where(r_i == c_i, img_row, 0), axis=1, keepdims=True)
    same = img_col == img_row
    rank_col = jnp.sum(jnp.where(same & (c_i < r_i), 1, 0), axis=1, keepdims=True)
    rank_row = jnp.sum(jnp.where(same & (r_i < c_i), 1, 0), axis=0, keepdims=True)
    slot_col = ((me - img_col + EXPERTS) & (EXPERTS - 1)) * 16 + rank_col
    slot_row = ((me - img_row + EXPERTS) & (EXPERTS - 1)) * 16 + rank_row
    for part in range(2):
        at = slice(part * CAP, (part + 1) * CAP)
        comp[at, :] = jnp.where(iota((CAP, SLOTS), 1) == slot_col + 8 * part, 1.0, 0.0).astype(BF16)
        comp_t[:, at] = jnp.where(iota((SLOTS, CAP), 0) == slot_row + 8 * part, 1.0, 0.0).astype(BF16)

    pick = jnp.where(iota((16, EXPERTS), 1) == me, 1.0, 0.0).astype(BF16)
    rw_row[...] = dot_nt(pick, rw_ref[...])[0:8]
    rw_e = rw_row[0:1, :]

    def compact(recv, out):
        for part in range(2):
            out[0:CAP, part * HALF : (part + 1) * HALF] = dot(
                comp[part * CAP : (part + 1) * CAP, :], recv[...]
            ).astype(BF16)

    def upstream(s):
        rows = slice(s * CAP, (s + 1) * CAP)

        def step(n, carry):
            cols = pl.ds(pl.multiple_of(n * TILE, TILE), TILE)
            up_scr[rows, cols] = dot_nt(g_all[rows, :], w_out[cols, :])
            return carry

        lax.fori_loop(0, HIDL // TILE, step, 0)

    def gates(s):
        rows = slice(s * CAP, (s + 1) * CAP)
        logits = jnp.sum(u_all[rows, :].astype(F32) * rw_e, axis=1, keepdims=True)
        q = jax.nn.sigmoid(logits).astype(BF16).astype(F32)
        q_all[rows, :] = jnp.broadcast_to(q, (CAP, 128))
        gy_all[rows, :] = (q * g_all[rows, :].astype(F32)).astype(BF16)

    def middle(s):
        rows = slice(s * CAP, (s + 1) * CAP)
        q = q_all[rows, 0:1]
        scores[rows, :] = jnp.zeros((CAP, 128), F32)

        def step(n, carry):
            cols = pl.ds(pl.multiple_of(n * TILE, TILE), TILE)
            a = dot(u_all[rows, :], w_in[:, cols])
            up = up_scr[rows, cols]
            a2 = a * a
            t = jnp.tanh(gelu_root * a * (1.0 + gelu_cube * a2))
            half = 0.5 * (1.0 + t)
            h = (a * half).astype(BF16)
            slope = half + (0.5 * gelu_root) * a * (1.0 - t * t) * (1.0 + (3.0 * gelu_cube) * a2)
            hid[rows, cols] = h
            gp[rows, cols] = (q * up * slope).astype(BF16)
            prod = h.astype(F32) * up
            scores[rows, :] += prod[:, 0:128] + prod[:, 128:256]
            return carry

        lax.fori_loop(0, HIDL // TILE, step, 0)
        score = jnp.sum(scores[rows, :], axis=1, keepdims=True)
        logit[rows, :] = jnp.broadcast_to(score * q * (1.0 - q), (CAP, 128))

    all_of(g_send, g_recv, 0, 16).wait_recv()
    compact(g_recv, g_all)
    to_partner(g_all.at[0:CAP], g_all.at[CAP:], 0).start()
    load_out.wait()
    upstream(0)

    all_of(u_send, u_recv, 1, 16).wait_recv()
    compact(u_recv, u_all)
    to_partner(u_all.at[0:CAP], u_all.at[CAP:], 1).start()
    load_in.wait()
    gates(0)
    middle(0)
    for part in range(2):
        at = slice(part * HALF, (part + 1) * HALF)
        own_part[part * CAP : (part + 1) * CAP, :] = (
            dot_nt(gp[0:CAP, :], w_in[at, :]) + logit[0:CAP, 0:1] * rw_e[:, at]
        )

    to_partner(g_all.at[0:CAP], g_all.at[CAP:], 0).wait()
    upstream(1)
    to_partner(u_all.at[0:CAP], u_all.at[CAP:], 1).wait()
    gates(1)
    middle(1)
    for part in range(2):
        at = slice(part * HALF, (part + 1) * HALF)
        rows = slice(part * CAP, (part + 1) * CAP)
        par_send[rows, :] = (
            dot_nt(gp[CAP:, :], w_in[at, :]) + logit[CAP:, 0:1] * rw_e[:, at]
        ).astype(BF16)
        to_partner(par_send.at[rows], par_recv.at[rows], 2 + part).start()

    column = jnp.sum(u_all[...].astype(F32) * logit[:, 0:1], axis=0, keepdims=True)
    for j in range(8):
        col_mine[j : j + 1, :] = column[:, j * 128 : (j + 1) * 128]
    to_partner(col_mine, col_theirs, 4).start()

    def grad_out_tile(n, carry):
        cols = pl.ds(pl.multiple_of(n * TILE, TILE), TILE)
        stage_out[cols, :] = dot_tn(hid[:, cols], gy_all[...]).astype(BF16)
        pltpu.make_async_copy(stage_out.at[cols], gwo_hbm.at[0, cols], out_sem.at[0]).start()
        return carry

    lax.fori_loop(0, HIDL // TILE, grad_out_tile, 0)

    to_partner(col_mine, col_theirs, 4).wait()
    total = col_mine[...] + col_theirs[...]
    col_sum[...] = total
    for part in range(2):
        rows = slice(part * CAP, (part + 1) * CAP)
        to_partner(par_send.at[rows], par_recv.at[rows], 2 + part).wait()
        own_part[rows, :] = own_part[rows, :] + par_recv[rows, :].astype(F32)
    back = own_part[...].astype(BF16)
    par_send[...] = back

    def spread_back(i, carry):
        rows = pl.ds(pl.multiple_of(i * TILE, TILE), TILE)
        ret_send[rows, :] = dot(comp_t[rows, :], par_send[...]).astype(BF16)
        return carry

    lax.fori_loop(0, SLOTS // TILE, spread_back, 0)
    send_all(ret_send, ret_recv, 2, -1, 16)
    ret_recv[0:16, :] = ret_send[0:16, :]

    def share_column(i, carry):
        pltpu.make_async_remote_copy(
            src_ref=col_sum,
            dst_ref=col_recv.at[pl.ds(pl.multiple_of(me * 8, 8), 8)],
            send_sem=send_sem.at[3],
            recv_sem=recv_sem.at[3],
            device_id=(d, (me + i) & (EXPERTS - 1)),
            device_id_type=MESH,
        ).start()
        return carry

    lax.fori_loop(1, EXPERTS, share_column, 0)

    def grad_in_tile(n, carry):
        cols = pl.ds(pl.multiple_of(n * TILE, TILE), TILE)
        stage_in[cols, :] = dot_tn(u_all[:, cols], gp[...]).astype(BF16)
        pltpu.make_async_copy(stage_in.at[cols], gwi_hbm.at[0, cols], out_sem.at[1]).start()
        return carry

    lax.fori_loop(0, WIDTH // TILE, grad_in_tile, 0)

    all_of(ret_send, ret_recv, 2, 16).wait_recv()
    for part in range(2):
        at = slice(part * HALF, (part + 1) * HALF)
        own_part[part * TOK : (part + 1) * TOK, :] = dot_tn(
            sel[:, part * TOK : (part + 1) * TOK], ret_recv[...]
        )
    mean_n = jnp.zeros((TOK, 1), F32)
    slope_n = jnp.zeros((TOK, 1), F32)
    for part in range(2):
        at = slice(part * HALF, (part + 1) * HALF)
        gu = own_part[part * TOK : (part + 1) * TOK, :]
        nr = normed[:, at]
        gn_n = gu * nr
        gm_ref[0, 0:1, at] = jnp.sum(gu, axis=0, keepdims=True)
        gm_ref[0, 1:2, at] = jnp.sum(gn_n, axis=0, keepdims=True)
        mean_n += jnp.sum(gu * scale[:, at], axis=1, keepdims=True)
        slope_n += jnp.sum(gn_n * scale[:, at], axis=1, keepdims=True)
    mean_n = mean_n * (1.0 / WIDTH)
    slope_n = slope_n * (1.0 / WIDTH)
    inv_t = inverse[:, 0:1]
    for part in range(2):
        at = slice(part * HALF, (part + 1) * HALF)
        gu = own_part[part * TOK : (part + 1) * TOK, :]
        gt_ref[:, at] = (
            go_ref[:, at].astype(F32)
            + (gu * scale[:, at] - mean_n - normed[:, at] * slope_n) * inv_t
        ).astype(BF16)

    all_of(g_send, g_recv, 0, 16).wait_send()
    all_of(u_send, u_recv, 1, 16).wait_send()
    all_of(ret_send, ret_recv, 2, 16).wait_send()
    column_wait = all_of(col_recv, col_recv, 3, 8)
    column_wait.wait_recv()
    column_wait.wait_send()
    col_recv[pl.ds(pl.multiple_of(me * 8, 8), 8), :] = col_sum[...]
    gr_ref[...] = col_recv[...]
    pltpu.make_async_copy(stage_out, gwo_hbm.at[0], out_sem.at[0]).wait()
    pltpu.make_async_copy(stage_in, gwi_hbm.at[0], out_sem.at[1]).wait()


def body(tokens, modulation, router_weight, weight_in, weight_out, chosen, grad_out):
    vmem = pl.BlockSpec(memory_space=pltpu.VMEM)
    hbm = pl.BlockSpec(memory_space=pl.ANY)
    sds = jax.ShapeDtypeStruct
    slots = pltpu.VMEM((SLOTS, HALF), BF16)
    rows = pltpu.VMEM((2 * CAP, WIDTH), BF16)
    inner = pltpu.VMEM((2 * CAP, HIDL), BF16)
    column = pltpu.VMEM((8, 128), F32)
    thin = pltpu.VMEM((2 * CAP, 128), F32)
    outs = pl.pallas_call(
        kernel,
        out_shape=(
            sds((TOK, WIDTH), BF16),
            sds((1, 2, WIDTH), F32),
            sds((EXPERTS * 8, 128), F32),
            sds((1, WIDTH, HIDL), BF16),
            sds((1, HIDL, WIDTH), BF16),
        ),
        in_specs=[vmem, vmem, vmem, hbm, hbm, vmem, vmem],
        out_specs=(vmem, vmem, vmem, hbm, hbm),
        scratch_shapes=[
            pltpu.VMEM((WIDTH, HIDL), BF16),
            pltpu.VMEM((HIDL, WIDTH), BF16),
            pltpu.VMEM((WIDTH, HIDL), BF16),
            pltpu.VMEM((HIDL, WIDTH), BF16),
            pltpu.VMEM((SLOTS, 2 * TOK), BF16),
            pltpu.VMEM((2 * CAP, SLOTS), BF16),
            pltpu.VMEM((SLOTS, 2 * CAP), BF16),
            slots, slots, slots, slots,
            rows, rows, rows,
            pltpu.VMEM((2 * CAP, HIDL), F32),
            inner, inner,
            pltpu.VMEM((2 * CAP, HALF), F32),
            pltpu.VMEM((2 * CAP, HALF), BF16),
            pltpu.VMEM((2 * CAP, HALF), BF16),
            slots, slots,
            pltpu.VMEM((2 * TOK, HALF), BF16),
            pltpu.VMEM((TOK, WIDTH), F32),
            pltpu.VMEM((TOK, 128), F32),
            thin, thin, thin,
            column, column, column,
            pltpu.VMEM((EXPERTS * 8, 128), F32),
            pltpu.VMEM((8, WIDTH), F32),
            pltpu.SemaphoreType.DMA((2,)),
            pltpu.SemaphoreType.DMA((2,)),
            pltpu.SemaphoreType.DMA((4,)),
            pltpu.SemaphoreType.DMA((4,)),
            pltpu.SemaphoreType.DMA((5,)),
            pltpu.SemaphoreType.DMA((5,)),
        ],
        compiler_params=pltpu.CompilerParams(
            collective_id=0, has_side_effects=True, vmem_limit_bytes=60 * 2**20
        ),
    )(tokens, modulation, router_weight, weight_in, weight_out, chosen, grad_out)
    grad_tokens, grad_mod, columns, grad_weight_in, grad_weight_out = outs
    grad_router = columns.reshape(EXPERTS, WIDTH).T
    return (grad_tokens, grad_mod, grad_router, grad_weight_in, grad_weight_out)


def solution(mesh):
    placed = (
        P(("dp", "expert"), None),
        P(("dp", "expert"), None, None),
        P(),
        P("expert", None, "dp"),
        P("expert", "dp", None),
        P("dp", None, None),
        P(("dp", "expert"), None),
    )
    return jax.shard_map(
        body,
        mesh=mesh,
        in_specs=placed,
        out_specs=(
            P(("dp", "expert"), None),
            P(("dp", "expert"), None, None),
            P(),
            P("expert", None, "dp"),
            P("expert", "dp", None),
        ),
        check_vma=False,
    )
```

```python
import jax
import jax.numpy as jnp
from jax import lax
from jax.experimental import pallas as pl
from jax.experimental.pallas import tpu as pltpu
from jax.sharding import PartitionSpec as P

gelu_root = 0.7978845608028654
gelu_cube = 0.044715
norm_eps = 1e-06

TOK = 256
WIDTH = 1024
HALF = 512
HIDL = 2048
EXPERTS = 64
CAP = 256
SLOTS = EXPERTS * 16
TILE = 256
F32 = jnp.float32
BF16 = jnp.bfloat16
MESH = pl.DeviceIdType.MESH


def iota(shape, dim):
    return lax.broadcasted_iota(jnp.int32, shape, dim)


def dot(a, b):
    return jnp.dot(a, b, preferred_element_type=F32)


def dot_nt(a, b):
    return lax.dot_general(a, b, (((1,), (1,)), ((), ())), preferred_element_type=F32)


def dot_tn(a, b):
    return lax.dot_general(a, b, (((0,), (0,)), ((), ())), preferred_element_type=F32)


def kernel(
    tok_ref, mod_ref, rw_ref, w_in_hbm, w_out_hbm, chosen_ref, go_ref,
    hid_hbm, gp_hbm, u_hbm, gy_hbm, norm_hbm, inverse, gu_ref, col_out,
    w_in, w_out, sel, comp, comp_t, comp_p,
    g_send, u_send, g_recv, u_recv, g_all, u_all, gy_all,
    up_scr, hid, gp, parts, ret_send, ret_recv, pret_send, pret_recv,
    halves, normed, scores, q_all, logit, col_mine, col_theirs, col_sum, col_recv, rw_row, list_mine, list_theirs,
    w_sem, out_sem, send_sem, recv_sem, pair_send, pair_recv,
):
    d = lax.axis_index("dp")
    me = lax.axis_index("expert")
    other = 1 - d

    load_out = pltpu.make_async_copy(w_out_hbm.at[0], w_out, w_sem.at[0])
    load_in = pltpu.make_async_copy(w_in_hbm.at[0], w_in, w_sem.at[1])
    load_out.start()
    load_in.start()

    barrier = pltpu.get_barrier_semaphore()

    def greet(step, carry):
        peer = (me + step) & (EXPERTS - 1)
        pl.semaphore_signal(barrier, inc=1, device_id=(d, peer), device_id_type=MESH)
        pl.semaphore_signal(barrier, inc=1, device_id=(other, peer), device_id_type=MESH)
        return carry

    pl.semaphore_signal(barrier, inc=1, device_id=(other, me), device_id_type=MESH)
    lax.fori_loop(1, EXPERTS, greet, 0)

    local = chosen_ref[0] - me * TOK
    mine = (local >= 0) & (local < TOK)
    before = jnp.where(iota((CAP, CAP), 0) < iota((CAP, CAP), 1), 1.0, 0.0).astype(BF16)
    rank = dot(jnp.where(mine, 1.0, 0.0).astype(BF16), before)
    local_f = (local + 1).astype(F32)
    lane = iota((EXPERTS, 128), 1)
    values = jnp.zeros((EXPERTS, 128), F32)
    for k in range(8):
        one = jnp.sum(
            jnp.where(mine & (rank == float(k)), local_f, 0.0), axis=1, keepdims=True
        )
        values = jnp.where(lane == k, one, values)
    values = values.astype(BF16)

    def fill_sel(i, carry):
        rows = pl.multiple_of(i * TILE, TILE)
        row = rows + iota((TILE, EXPERTS), 0)
        expert = ((row >> 4) + me) & (EXPERTS - 1)
        spread = dot(jnp.where(expert == iota((TILE, EXPERTS), 1), 1.0, 0.0).astype(BF16), values)
        row_k = iota((TILE, 128), 0) & 7
        token = jnp.sum(
            jnp.where(row_k == iota((TILE, 128), 1), spread, 0.0), axis=1, keepdims=True
        )
        part = ((iota((TILE, 1), 0) >> 3) & 1).astype(F32) * float(TOK)
        target = jnp.where(token > 0.5, token - 1.0 + part, -1.0)
        sel[pl.ds(rows, TILE), :] = jnp.where(
            iota((TILE, 2 * TOK), 1).astype(F32) == target, 1.0, 0.0
        ).astype(BF16)
        return carry

    lax.fori_loop(0, SLOTS // TILE, fill_sel, 0)

    def spread_rows(out):
        def step(i, carry):
            rows = pl.multiple_of(i * TILE, TILE)
            out[pl.ds(rows, TILE), :] = dot(sel[pl.ds(rows, TILE), :], halves[...]).astype(BF16)
            return carry

        lax.fori_loop(0, SLOTS // TILE, step, 0)

    def send_all(src, dst, which, sign, size, to, first):
        def step(i, carry):
            rows = pl.ds(pl.multiple_of(i * size, size), size)
            pltpu.make_async_remote_copy(
                src_ref=src.at[rows],
                dst_ref=dst.at[rows],
                send_sem=send_sem.at[which],
                recv_sem=recv_sem.at[which],
                device_id=(to, (me + sign * i + EXPERTS) & (EXPERTS - 1)),
                device_id_type=MESH,
            ).start()
            return carry

        lax.fori_loop(first, EXPERTS, step, 0)

    def all_of(src, dst, which, size, first):
        rows = pl.ds(first * size, (EXPERTS - first) * size)
        return pltpu.make_async_remote_copy(
            src_ref=src.at[rows],
            dst_ref=dst.at[rows],
            send_sem=send_sem.at[which],
            recv_sem=recv_sem.at[which],
            device_id=(d, (me + 1) & (EXPERTS - 1)),
            device_id_type=MESH,
        )

    def keep(src, dst, which):
        return pltpu.make_async_copy(src, dst, out_sem.at[which])

    def to_partner(src, dst, which):
        return pltpu.make_async_remote_copy(
            src_ref=src,
            dst_ref=dst,
            send_sem=pair_send.at[which],
            recv_sem=pair_recv.at[which],
            device_id=(other, me),
            device_id_type=MESH,
        )

    halves[0:TOK, :] = go_ref[:, 0:HALF]
    halves[TOK:, :] = go_ref[:, HALF:]
    spread_rows(g_send)
    pl.semaphore_wait(barrier, 2 * EXPERTS - 1)
    send_all(g_send, g_recv, 0, 1, 16, d, 1)
    one_row = chosen_ref[0, pl.ds(me, 1), :]
    list_mine[...] = jnp.broadcast_to(one_row, (8, CAP))
    to_partner(list_mine, list_theirs, 2).start()
    g_recv[0:16, :] = g_send[0:16, :]

    shift = mod_ref[0, 0:1, :].astype(F32)
    scale = 1.0 + mod_ref[0, 1:2, :].astype(F32)
    x = tok_ref[...].astype(F32)
    centred = x - jnp.mean(x, axis=1, keepdims=True)
    inv = lax.rsqrt(jnp.mean(centred * centred, axis=1, keepdims=True) + norm_eps)
    nrm = centred * inv
    normed[...] = nrm
    keep(normed, norm_hbm, 0).start()
    inverse[...] = jnp.broadcast_to(inv, (TOK, 128))
    u = (nrm * scale + shift).astype(BF16)
    halves[0:TOK, :] = u[:, 0:HALF]
    halves[TOK:, :] = u[:, HALF:]
    spread_rows(u_send)
    send_all(u_send, u_recv, 1, 1, 16, d, 1)
    u_recv[0:16, :] = u_send[0:16, :]

    r_i, c_i = iota((CAP, CAP), 0), iota((CAP, CAP), 1)

    def places(row):
        img_row = row >> 8
        img_col = jnp.sum(jnp.where(r_i == c_i, img_row, 0), axis=1, keepdims=True)
        same = img_col == img_row
        rank_row = jnp.sum(jnp.where(same & (r_i < c_i), 1, 0), axis=0, keepdims=True)
        slot_row = ((me - img_row + EXPERTS) & (EXPERTS - 1)) * 16 + rank_row
        return img_col, same, slot_row

    def fill_back(slot_row, out):
        for part in range(2):
            out[:, part * CAP : (part + 1) * CAP] = jnp.where(
                iota((SLOTS, CAP), 0) == slot_row + 8 * part, 1.0, 0.0
            ).astype(BF16)

    img_col, same, slot_row = places(one_row)
    rank_col = jnp.sum(jnp.where(same & (c_i < r_i), 1, 0), axis=1, keepdims=True)
    slot_col = ((me - img_col + EXPERTS) & (EXPERTS - 1)) * 16 + rank_col
    for part in range(2):
        comp[part * CAP : (part + 1) * CAP, :] = jnp.where(
            iota((CAP, SLOTS), 1) == slot_col + 8 * part, 1.0, 0.0
        ).astype(BF16)
    fill_back(slot_row, comp_t)
    to_partner(list_mine, list_theirs, 2).wait()
    fill_back(places(list_theirs[0:1, :])[2], comp_p)

    pick = jnp.where(iota((16, EXPERTS), 1) == me, 1.0, 0.0).astype(BF16)
    rw_row[...] = dot(pick, rw_ref[...])[0:8]
    rw_e = rw_row[0:1, :]

    def compact(recv, out):
        for part in range(2):
            out[0:CAP, part * HALF : (part + 1) * HALF] = dot(
                comp[part * CAP : (part + 1) * CAP, :], recv[...]
            ).astype(BF16)

    def upstream(s):
        rows = slice(s * CAP, (s + 1) * CAP)

        def step(n, carry):
            cols = pl.ds(pl.multiple_of(n * TILE, TILE), TILE)
            up_scr[rows, cols] = dot_nt(g_all[rows, :], w_out[cols, :])
            return carry

        lax.fori_loop(0, HIDL // TILE, step, 0)

    def gates(s):
        rows = slice(s * CAP, (s + 1) * CAP)
        logits = jnp.sum(u_all[rows, :].astype(F32) * rw_e, axis=1, keepdims=True)
        q = jax.nn.sigmoid(logits).astype(BF16).astype(F32)
        q_all[rows, :] = jnp.broadcast_to(q, (CAP, 128))
        gy_all[rows, :] = (q * g_all[rows, :].astype(F32)).astype(BF16)

    def middle(s):
        rows = slice(s * CAP, (s + 1) * CAP)
        q = q_all[rows, 0:1]
        scores[rows, :] = jnp.zeros((CAP, 128), F32)

        def step(n, carry):
            cols = pl.ds(pl.multiple_of(n * TILE, TILE), TILE)
            a = dot(u_all[rows, :], w_in[:, cols])
            up = up_scr[rows, cols]
            a2 = a * a
            t = jnp.tanh(gelu_root * a * (1.0 + gelu_cube * a2))
            half = 0.5 * (1.0 + t)
            h = (a * half).astype(BF16)
            slope = half + (0.5 * gelu_root) * a * (1.0 - t * t) * (1.0 + (3.0 * gelu_cube) * a2)
            hid[rows, cols] = h
            gp[rows, cols] = (q * up * slope).astype(BF16)
            prod = h.astype(F32) * up
            scores[rows, :] += prod[:, 0:128] + prod[:, 128:256]
            return carry

        lax.fori_loop(0, HIDL // TILE, step, 0)
        score = jnp.sum(scores[rows, :], axis=1, keepdims=True)
        logit[rows, :] = jnp.broadcast_to(score * q * (1.0 - q), (CAP, 128))

    def row_gradients(s, places_t, send):
        rows = slice(s * CAP, (s + 1) * CAP)
        for part in range(2):
            at = slice(part * HALF, (part + 1) * HALF)
            parts[part * CAP : (part + 1) * CAP, :] = (
                dot_nt(gp[rows, :], w_in[at, :]) + logit[rows, 0:1] * rw_e[:, at]
            ).astype(BF16)

        def step(i, carry):
            slots = pl.ds(pl.multiple_of(i * TILE, TILE), TILE)
            send[slots, :] = dot(places_t[slots, :], parts[...]).astype(BF16)
            return carry

        lax.fori_loop(0, SLOTS // TILE, step, 0)

    all_of(g_send, g_recv, 0, 16, 1).wait_recv()
    compact(g_recv, g_all)
    to_partner(g_all.at[0:CAP], g_all.at[CAP:], 0).start()
    load_out.wait()
    upstream(0)

    all_of(u_send, u_recv, 1, 16, 1).wait_recv()
    compact(u_recv, u_all)
    to_partner(u_all.at[0:CAP], u_all.at[CAP:], 1).start()
    load_in.wait()
    gates(0)
    middle(0)
    row_gradients(0, comp_t, ret_send)
    send_all(ret_send, ret_recv, 2, -1, 16, d, 1)
    ret_recv[0:16, :] = ret_send[0:16, :]

    to_partner(g_all.at[0:CAP], g_all.at[CAP:], 0).wait()
    upstream(1)
    to_partner(u_all.at[0:CAP], u_all.at[CAP:], 1).wait()
    gates(1)
    middle(1)
    row_gradients(1, comp_p, pret_send)
    send_all(pret_send, pret_recv, 4, -1, 16, other, 0)
    keep(hid, hid_hbm, 1).start()
    keep(gp, gp_hbm, 2).start()
    keep(u_all, u_hbm, 3).start()
    keep(gy_all, gy_hbm, 4).start()

    column = jnp.sum(u_all[...].astype(F32) * logit[:, 0:1], axis=0, keepdims=True)
    for j in range(8):
        col_mine[j : j + 1, :] = column[:, j * 128 : (j + 1) * 128]
    to_partner(col_mine, col_theirs, 3).start()
    to_partner(col_mine, col_theirs, 3).wait()
    col_sum[...] = col_mine[...] + col_theirs[...]

    def share_column(i, carry):
        pltpu.make_async_remote_copy(
            src_ref=col_sum,
            dst_ref=col_recv.at[pl.ds(pl.multiple_of(me * 8, 8), 8)],
            send_sem=send_sem.at[3],
            recv_sem=recv_sem.at[3],
            device_id=(d, (me + i) & (EXPERTS - 1)),
            device_id_type=MESH,
        ).start()
        return carry

    lax.fori_loop(1, EXPERTS, share_column, 0)
    all_of(g_send, g_recv, 0, 16, 1).wait_send()
    all_of(u_send, u_recv, 1, 16, 1).wait_send()

    def gather_back(recv, first):
        for part in range(2):
            rows = slice(part * TOK, (part + 1) * TOK)
            back = dot_tn(sel[:, rows], recv[...])
            gu_ref[rows, :] = back if first else gu_ref[rows, :] + back

    all_of(ret_send, ret_recv, 2, 16, 1).wait()
    gather_back(ret_recv, True)
    column_wait = all_of(col_recv, col_recv, 3, 8, 1)
    column_wait.wait_recv()
    column_wait.wait_send()
    col_recv[pl.ds(pl.multiple_of(me * 8, 8), 8), :] = col_sum[...]
    col_out[...] = col_recv[...]
    all_of(pret_send, pret_recv, 4, 16, 0).wait()
    gather_back(pret_recv, False)
    keep(normed, norm_hbm, 0).wait()
    keep(hid, hid_hbm, 1).wait()
    keep(gp, gp_hbm, 2).wait()
    keep(u_all, u_hbm, 3).wait()
    keep(gy_all, gy_hbm, 4).wait()


def finish(
    hid_hbm, gp_hbm, u_hbm, gy_hbm, norm_hbm, gu_hbm, go_hbm, inverse, mod_ref, col_ref,
    gt_ref, gm_ref, gr_ref, gwi_hbm, gwo_hbm,
    hid, gp, u_all, gy_all, normed, gu_all, go, stage_in, stage_out, sem, out_sem,
):
    loads = [
        pltpu.make_async_copy(src, dst, sem.at[i])
        for i, (src, dst) in enumerate(
            (
                (gy_hbm, gy_all), (hid_hbm, hid), (u_hbm, u_all), (gp_hbm, gp),
                (gu_hbm, gu_all), (norm_hbm, normed), (go_hbm, go),
            )
        )
    ]
    for load in loads:
        load.start()
    for j in range(8):
        gr_ref[:, j * 128 : (j + 1) * 128] = col_ref[:, j, :]
    loads[0].wait()
    loads[1].wait()

    def grad_out_tile(n, carry):
        cols = pl.ds(pl.multiple_of(n * TILE, TILE), TILE)
        stage_out[cols, :] = dot_tn(hid[:, cols], gy_all[...]).astype(BF16)
        pltpu.make_async_copy(stage_out.at[cols], gwo_hbm.at[0, cols], out_sem.at[0]).start()
        return carry

    lax.fori_loop(0, HIDL // TILE, grad_out_tile, 0)
    loads[2].wait()
    loads[3].wait()

    def grad_in_tile(n, carry):
        cols = pl.ds(pl.multiple_of(n * TILE, TILE), TILE)
        stage_in[cols, :] = dot_tn(u_all[:, cols], gp[...]).astype(BF16)
        pltpu.make_async_copy(stage_in.at[cols], gwi_hbm.at[0, cols], out_sem.at[1]).start()
        return carry

    lax.fori_loop(0, WIDTH // TILE, grad_in_tile, 0)
    for load in loads[4:]:
        load.wait()

    scale = 1.0 + mod_ref[0, 1:2, :].astype(F32)
    mean_n = jnp.zeros((TOK, 1), F32)
    slope_n = jnp.zeros((TOK, 1), F32)
    for part in range(2):
        at = slice(part * HALF, (part + 1) * HALF)
        gu = gu_all[part * TOK : (part + 1) * TOK, :]
        gn_n = gu * normed[:, at]
        gm_ref[0, 0:1, at] = jnp.sum(gu, axis=0, keepdims=True)
        gm_ref[0, 1:2, at] = jnp.sum(gn_n, axis=0, keepdims=True)
        mean_n += jnp.sum(gu * scale[:, at], axis=1, keepdims=True)
        slope_n += jnp.sum(gn_n * scale[:, at], axis=1, keepdims=True)
    mean_n = mean_n * (1.0 / WIDTH)
    slope_n = slope_n * (1.0 / WIDTH)
    inv_t = inverse[:, 0:1]
    for part in range(2):
        at = slice(part * HALF, (part + 1) * HALF)
        gu = gu_all[part * TOK : (part + 1) * TOK, :]
        gt_ref[:, at] = (
            go[:, at].astype(F32)
            + (gu * scale[:, at] - mean_n - normed[:, at] * slope_n) * inv_t
        ).astype(BF16)
    pltpu.make_async_copy(stage_out, gwo_hbm.at[0], out_sem.at[0]).wait()
    pltpu.make_async_copy(stage_in, gwi_hbm.at[0], out_sem.at[1]).wait()


def body(tokens, modulation, router_weight, weight_in, weight_out, chosen, grad_out):
    vmem = pl.BlockSpec(memory_space=pltpu.VMEM)
    hbm = pl.BlockSpec(memory_space=pl.ANY)
    sds = jax.ShapeDtypeStruct
    slots = pltpu.VMEM((SLOTS, HALF), BF16)
    rows = pltpu.VMEM((2 * CAP, WIDTH), BF16)
    inner = pltpu.VMEM((2 * CAP, HIDL), BF16)
    column = pltpu.VMEM((8, 128), F32)
    thin = pltpu.VMEM((2 * CAP, 128), F32)
    params = dict(vmem_limit_bytes=60 * 2**20)
    hid, gp, u_all, gy_all, normed, inverse, gu, columns = pl.pallas_call(
        kernel,
        out_shape=(
            sds((2 * CAP, HIDL), BF16),
            sds((2 * CAP, HIDL), BF16),
            sds((2 * CAP, WIDTH), BF16),
            sds((2 * CAP, WIDTH), BF16),
            sds((TOK, WIDTH), F32),
            sds((TOK, 128), F32),
            sds((2 * TOK, HALF), F32),
            sds((EXPERTS * 8, 128), F32),
        ),
        in_specs=[vmem, vmem, vmem, hbm, hbm, vmem, vmem],
        out_specs=(hbm, hbm, hbm, hbm, hbm, vmem, vmem, vmem),
        scratch_shapes=[
            pltpu.VMEM((WIDTH, HIDL), BF16),
            pltpu.VMEM((HIDL, WIDTH), BF16),
            pltpu.VMEM((SLOTS, 2 * TOK), BF16),
            pltpu.VMEM((2 * CAP, SLOTS), BF16),
            pltpu.VMEM((SLOTS, 2 * CAP), BF16),
            pltpu.VMEM((SLOTS, 2 * CAP), BF16),
            slots, slots, slots, slots,
            rows, rows, rows,
            pltpu.VMEM((2 * CAP, HIDL), F32),
            inner, inner,
            pltpu.VMEM((2 * CAP, HALF), BF16),
            slots, slots, slots, slots,
            pltpu.VMEM((2 * TOK, HALF), BF16),
            pltpu.VMEM((TOK, WIDTH), F32),
            thin, thin, thin,
            column, column, column,
            pltpu.VMEM((EXPERTS * 8, 128), F32),
            pltpu.VMEM((8, WIDTH), F32),
            pltpu.VMEM((8, CAP), jnp.int32),
            pltpu.VMEM((8, CAP), jnp.int32),
            pltpu.SemaphoreType.DMA((2,)),
            pltpu.SemaphoreType.DMA((5,)),
            pltpu.SemaphoreType.DMA((5,)),
            pltpu.SemaphoreType.DMA((5,)),
            pltpu.SemaphoreType.DMA((4,)),
            pltpu.SemaphoreType.DMA((4,)),
        ],
        compiler_params=pltpu.CompilerParams(collective_id=0, has_side_effects=True, **params),
    )(tokens, modulation, router_weight.T, weight_in, weight_out, chosen, grad_out)
    grad_tokens, grad_mod, columns, grad_weight_in, grad_weight_out = pl.pallas_call(
        finish,
        out_shape=(
            sds((TOK, WIDTH), BF16),
            sds((1, 2, WIDTH), F32),
            sds((EXPERTS, WIDTH), F32),
            sds((1, WIDTH, HIDL), BF16),
            sds((1, HIDL, WIDTH), BF16),
        ),
        in_specs=[hbm] * 7 + [vmem] * 3,
        out_specs=(vmem, vmem, vmem, hbm, hbm),
        scratch_shapes=[
            inner, inner, rows, rows,
            pltpu.VMEM((TOK, WIDTH), F32),
            pltpu.VMEM((2 * TOK, HALF), F32),
            pltpu.VMEM((TOK, WIDTH), BF16),
            pltpu.VMEM((WIDTH, HIDL), BF16),
            pltpu.VMEM((HIDL, WIDTH), BF16),
            pltpu.SemaphoreType.DMA((7,)),
            pltpu.SemaphoreType.DMA((2,)),
        ],
        compiler_params=pltpu.CompilerParams(**params),
    )(
        hid, gp, u_all, gy_all, normed, gu, grad_out, inverse, modulation,
        columns.reshape(EXPERTS, 8, 128),
    )
    return (grad_tokens, grad_mod, columns.T, grad_weight_in, grad_weight_out)


def solution(mesh):
    placed = (
        P(("dp", "expert"), None),
        P(("dp", "expert"), None, None),
        P(),
        P("expert", None, "dp"),
        P("expert", "dp", None),
        P("dp", None, None),
        P(("dp", "expert"), None),
    )
    return jax.shard_map(
        body,
        mesh=mesh,
        in_specs=placed,
        out_specs=(
            P(("dp", "expert"), None),
            P(("dp", "expert"), None, None),
            P(),
            P("expert", None, "dp"),
            P("expert", "dp", None),
        ),
        check_vma=False,
    )
```

```python
import jax
import jax.numpy as jnp
from jax import lax
from jax.experimental import pallas as pl
from jax.experimental.pallas import tpu as pltpu
from jax.sharding import PartitionSpec as P

gelu_root = 0.7978845608028654
gelu_cube = 0.044715
norm_eps = 1e-06

TOK = 256
WIDTH = 1024
HALF = 512
HIDL = 2048
EXPERTS = 64
CAP = 256
SLOTS = EXPERTS * 16
TILE = 256
STEP = 21
STEP_INV = 61
F32 = jnp.float32
BF16 = jnp.bfloat16
MESH = pl.DeviceIdType.MESH


def iota(shape, dim):
    return lax.broadcasted_iota(jnp.int32, shape, dim)


def dot(a, b):
    return jnp.dot(a, b, preferred_element_type=F32)


def dot_nt(a, b):
    return lax.dot_general(a, b, (((1,), (1,)), ((), ())), preferred_element_type=F32)


def dot_tn(a, b):
    return lax.dot_general(a, b, (((0,), (0,)), ((), ())), preferred_element_type=F32)


def kernel(
    tok_ref, mod_ref, rw_ref, w_in_hbm, w_out_hbm, chosen_ref, go_ref,
    stage, stage_in, norm_hbm, inverse, gu_ref, col_out,
    w_in, w_out, sel, comp, comp_t, comp_p,
    g_send, u_send, g_recv, u_recv, g_all, u_all, gy_all,
    up_scr, hid, gp, parts, ret_send, ret_recv, pret_send, pret_recv,
    halves, normed, scores, q_all, logit, col_mine, col_theirs, col_sum, col_recv, rw_row, list_mine, list_theirs,
    w_sem, out_sem, send_sem, recv_sem, pair_send, pair_recv,
):
    d = lax.axis_index("dp")
    me = lax.axis_index("expert")
    other = 1 - d

    load_out = pltpu.make_async_copy(w_out_hbm.at[0], w_out, w_sem.at[0])
    load_in = pltpu.make_async_copy(w_in_hbm.at[0], w_in, w_sem.at[1])
    load_out.start()
    load_in.start()

    barrier = pltpu.get_barrier_semaphore()

    def greet(step, carry):
        peer = (me + step) & (EXPERTS - 1)
        pl.semaphore_signal(barrier, inc=1, device_id=(d, peer), device_id_type=MESH)
        pl.semaphore_signal(barrier, inc=1, device_id=(other, peer), device_id_type=MESH)
        return carry

    pl.semaphore_signal(barrier, inc=1, device_id=(other, me), device_id_type=MESH)
    lax.fori_loop(1, EXPERTS, greet, 0)

    local = chosen_ref[0] - me * TOK
    mine = (local >= 0) & (local < TOK)
    before = jnp.where(iota((CAP, CAP), 0) < iota((CAP, CAP), 1), 1.0, 0.0).astype(BF16)
    rank = dot(jnp.where(mine, 1.0, 0.0).astype(BF16), before)
    local_f = (local + 1).astype(F32)
    lane = iota((EXPERTS, 128), 1)
    values = jnp.zeros((EXPERTS, 128), F32)
    for k in range(8):
        one = jnp.sum(
            jnp.where(mine & (rank == float(k)), local_f, 0.0), axis=1, keepdims=True
        )
        values = jnp.where(lane == k, one, values)
    values = values.astype(BF16)

    def fill_sel(i, carry):
        rows = pl.multiple_of(i * TILE, TILE)
        row = rows + iota((TILE, EXPERTS), 0)
        expert = ((row >> 4) * STEP + me) & (EXPERTS - 1)
        spread = dot(jnp.where(expert == iota((TILE, EXPERTS), 1), 1.0, 0.0).astype(BF16), values)
        row_k = iota((TILE, 128), 0) & 7
        token = jnp.sum(
            jnp.where(row_k == iota((TILE, 128), 1), spread, 0.0), axis=1, keepdims=True
        )
        part = ((iota((TILE, 1), 0) >> 3) & 1).astype(F32) * float(TOK)
        target = jnp.where(token > 0.5, token - 1.0 + part, -1.0)
        sel[pl.ds(rows, TILE), :] = jnp.where(
            iota((TILE, 2 * TOK), 1).astype(F32) == target, 1.0, 0.0
        ).astype(BF16)
        return carry

    lax.fori_loop(0, SLOTS // TILE, fill_sel, 0)

    def spread_rows(out):
        def step(i, carry):
            rows = pl.multiple_of(i * TILE, TILE)
            out[pl.ds(rows, TILE), :] = dot(sel[pl.ds(rows, TILE), :], halves[...]).astype(BF16)
            return carry

        lax.fori_loop(0, SLOTS // TILE, step, 0)

    def send_all(src, dst, which, sign, size, to, first):
        def step(i, carry):
            rows = pl.ds(pl.multiple_of(i * size, size), size)
            pltpu.make_async_remote_copy(
                src_ref=src.at[rows],
                dst_ref=dst.at[rows],
                send_sem=send_sem.at[which],
                recv_sem=recv_sem.at[which],
                device_id=(to, (me + (sign * STEP) % EXPERTS * i) & (EXPERTS - 1)),
                device_id_type=MESH,
            ).start()
            return carry

        lax.fori_loop(first, EXPERTS, step, 0)

    def all_of(src, dst, which, size, first):
        rows = pl.ds(first * size, (EXPERTS - first) * size)
        return pltpu.make_async_remote_copy(
            src_ref=src.at[rows],
            dst_ref=dst.at[rows],
            send_sem=send_sem.at[which],
            recv_sem=recv_sem.at[which],
            device_id=(d, (me + 1) & (EXPERTS - 1)),
            device_id_type=MESH,
        )

    def keep(src, dst, which):
        return pltpu.make_async_copy(src, dst, out_sem.at[which])

    def to_partner(src, dst, which):
        return pltpu.make_async_remote_copy(
            src_ref=src,
            dst_ref=dst,
            send_sem=pair_send.at[which],
            recv_sem=pair_recv.at[which],
            device_id=(other, me),
            device_id_type=MESH,
        )

    halves[0:TOK, :] = go_ref[:, 0:HALF]
    halves[TOK:, :] = go_ref[:, HALF:]
    spread_rows(g_send)
    pl.semaphore_wait(barrier, 2 * EXPERTS - 1)
    send_all(g_send, g_recv, 0, 1, 16, d, 1)
    one_row = chosen_ref[0, pl.ds(me, 1), :]
    list_mine[...] = jnp.broadcast_to(one_row, (8, CAP))
    to_partner(list_mine, list_theirs, 2).start()
    g_recv[0:16, :] = g_send[0:16, :]

    shift = mod_ref[0, 0:1, :].astype(F32)
    scale = 1.0 + mod_ref[0, 1:2, :].astype(F32)
    x = tok_ref[...].astype(F32)
    centred = x - jnp.mean(x, axis=1, keepdims=True)
    inv = lax.rsqrt(jnp.mean(centred * centred, axis=1, keepdims=True) + norm_eps)
    nrm = centred * inv
    normed[...] = nrm
    keep(normed, norm_hbm, 0).start()
    inverse[...] = jnp.broadcast_to(inv, (TOK, 128))
    u = (nrm * scale + shift).astype(BF16)
    halves[0:TOK, :] = u[:, 0:HALF]
    halves[TOK:, :] = u[:, HALF:]
    spread_rows(u_send)
    send_all(u_send, u_recv, 1, 1, 16, d, 1)
    u_recv[0:16, :] = u_send[0:16, :]

    r_i, c_i = iota((CAP, CAP), 0), iota((CAP, CAP), 1)

    def places(row):
        img_row = row >> 8
        img_col = jnp.sum(jnp.where(r_i == c_i, img_row, 0), axis=1, keepdims=True)
        same = img_col == img_row
        rank_row = jnp.sum(jnp.where(same & (r_i < c_i), 1, 0), axis=0, keepdims=True)
        slot_row = (((me - img_row + EXPERTS) * STEP_INV) & (EXPERTS - 1)) * 16 + rank_row
        return img_col, same, slot_row

    def fill_back(slot_row, out):
        for part in range(2):
            out[:, part * CAP : (part + 1) * CAP] = jnp.where(
                iota((SLOTS, CAP), 0) == slot_row + 8 * part, 1.0, 0.0
            ).astype(BF16)

    img_col, same, slot_row = places(one_row)
    rank_col = jnp.sum(jnp.where(same & (c_i < r_i), 1, 0), axis=1, keepdims=True)
    slot_col = (((me - img_col + EXPERTS) * STEP_INV) & (EXPERTS - 1)) * 16 + rank_col
    for part in range(2):
        comp[part * CAP : (part + 1) * CAP, :] = jnp.where(
            iota((CAP, SLOTS), 1) == slot_col + 8 * part, 1.0, 0.0
        ).astype(BF16)
    fill_back(slot_row, comp_t)
    to_partner(list_mine, list_theirs, 2).wait()
    fill_back(places(list_theirs[0:1, :])[2], comp_p)

    pick = jnp.where(iota((16, EXPERTS), 1) == me, 1.0, 0.0).astype(BF16)
    rw_row[...] = dot(pick, rw_ref[...])[0:8]
    rw_e = rw_row[0:1, :]

    def compact(recv, out):
        for part in range(2):
            out[0:CAP, part * HALF : (part + 1) * HALF] = dot(
                comp[part * CAP : (part + 1) * CAP, :], recv[...]
            ).astype(BF16)

    def upstream(s):
        rows = slice(s * CAP, (s + 1) * CAP)

        def step(n, carry):
            cols = pl.ds(pl.multiple_of(n * TILE, TILE), TILE)
            up_scr[rows, cols] = dot_nt(g_all[rows, :], w_out[cols, :])
            return carry

        lax.fori_loop(0, HIDL // TILE, step, 0, unroll=4)

    def gates(s):
        rows = slice(s * CAP, (s + 1) * CAP)
        logits = jnp.sum(u_all[rows, :].astype(F32) * rw_e, axis=1, keepdims=True)
        q = jax.nn.sigmoid(logits).astype(BF16).astype(F32)
        q_all[rows, :] = jnp.broadcast_to(q, (CAP, 128))
        gy_all[rows, :] = (q * g_all[rows, :].astype(F32)).astype(BF16)

    def middle(s):
        rows = slice(s * CAP, (s + 1) * CAP)
        q = q_all[rows, 0:1]
        scores[rows, :] = jnp.zeros((CAP, 128), F32)

        def step(n, carry):
            cols = pl.ds(pl.multiple_of(n * TILE, TILE), TILE)
            a = dot(u_all[rows, :], w_in[:, cols])
            up = up_scr[rows, cols]
            a2 = a * a
            t = jnp.tanh(gelu_root * a * (1.0 + gelu_cube * a2))
            half = 0.5 * (1.0 + t)
            h = (a * half).astype(BF16)
            slope = half + (0.5 * gelu_root) * a * (1.0 - t * t) * (1.0 + (3.0 * gelu_cube) * a2)
            hid[rows, cols] = h
            gp[rows, cols] = (q * up * slope).astype(BF16)
            prod = h.astype(F32) * up
            scores[rows, :] += prod[:, 0:128] + prod[:, 128:256]
            return carry

        lax.fori_loop(0, HIDL // TILE, step, 0, unroll=4)
        score = jnp.sum(scores[rows, :], axis=1, keepdims=True)
        logit[rows, :] = jnp.broadcast_to(score * q * (1.0 - q), (CAP, 128))

    def row_gradients(s, places_t, send):
        rows = slice(s * CAP, (s + 1) * CAP)
        for part in range(2):
            at = slice(part * HALF, (part + 1) * HALF)
            parts[part * CAP : (part + 1) * CAP, :] = (
                dot_nt(gp[rows, :], w_in[at, :]) + logit[rows, 0:1] * rw_e[:, at]
            ).astype(BF16)

        def step(i, carry):
            slots = pl.ds(pl.multiple_of(i * TILE, TILE), TILE)
            send[slots, :] = dot(places_t[slots, :], parts[...]).astype(BF16)
            return carry

        lax.fori_loop(0, SLOTS // TILE, step, 0)

    all_of(g_send, g_recv, 0, 16, 1).wait_recv()
    compact(g_recv, g_all)
    to_partner(g_all.at[0:CAP], g_all.at[CAP:], 0).start()
    load_out.wait()
    upstream(0)

    all_of(u_send, u_recv, 1, 16, 1).wait_recv()
    compact(u_recv, u_all)
    to_partner(u_all.at[0:CAP], u_all.at[CAP:], 1).start()
    to_partner(g_all.at[0:CAP], g_all.at[CAP:], 0).wait()
    upstream(1)
    load_in.wait()
    gates(0)
    middle(0)
    row_gradients(0, comp_t, ret_send)
    send_all(ret_send, ret_recv, 2, -1, 16, d, 1)
    ret_recv[0:16, :] = ret_send[0:16, :]

    to_partner(u_all.at[0:CAP], u_all.at[CAP:], 1).wait()
    gates(1)
    middle(1)
    row_gradients(1, comp_p, pret_send)
    send_all(pret_send, pret_recv, 4, -1, 16, other, 0)

    column = jnp.sum(u_all[...].astype(F32) * logit[:, 0:1], axis=0, keepdims=True)
    for j in range(8):
        col_mine[j : j + 1, :] = column[:, j * 128 : (j + 1) * 128]
    to_partner(col_mine, col_theirs, 3).start()

    def grad_out_tile(n, carry):
        cols = pl.ds(pl.multiple_of(n * TILE, TILE), TILE)
        stage[cols, :] = dot_tn(hid[:, cols], gy_all[...]).astype(BF16)
        return carry

    lax.fori_loop(0, HIDL // TILE, grad_out_tile, 0)
    to_partner(col_mine, col_theirs, 3).wait()
    col_sum[...] = col_mine[...] + col_theirs[...]

    def share_column(i, carry):
        pltpu.make_async_remote_copy(
            src_ref=col_sum,
            dst_ref=col_recv.at[pl.ds(pl.multiple_of(me * 8, 8), 8)],
            send_sem=send_sem.at[3],
            recv_sem=recv_sem.at[3],
            device_id=(d, (me + STEP * i) & (EXPERTS - 1)),
            device_id_type=MESH,
        ).start()
        return carry

    lax.fori_loop(1, EXPERTS, share_column, 0)

    def grad_in_tile(n, carry):
        cols = pl.ds(pl.multiple_of(n * TILE, TILE), TILE)
        stage_in[cols, :] = dot_tn(u_all[:, cols], gp[...]).astype(BF16)
        return carry

    lax.fori_loop(0, WIDTH // TILE, grad_in_tile, 0)
    all_of(g_send, g_recv, 0, 16, 1).wait_send()
    all_of(u_send, u_recv, 1, 16, 1).wait_send()

    def gather_back(recv, first):
        for part in range(2):
            rows = slice(part * TOK, (part + 1) * TOK)
            back = dot_tn(sel[:, rows], recv[...])
            gu_ref[rows, :] = back if first else gu_ref[rows, :] + back

    all_of(ret_send, ret_recv, 2, 16, 1).wait()
    gather_back(ret_recv, True)
    column_wait = all_of(col_recv, col_recv, 3, 8, 1)
    column_wait.wait_recv()
    column_wait.wait_send()
    col_recv[pl.ds(pl.multiple_of(me * 8, 8), 8), :] = col_sum[...]
    col_out[...] = col_recv[...]
    all_of(pret_send, pret_recv, 4, 16, 0).wait()
    gather_back(pret_recv, False)
    keep(normed, norm_hbm, 0).wait()


def finish(
    gwo_made, gwi_made, norm_hbm, gu_hbm, go_hbm, inverse, mod_ref, col_ref,
    gt_ref, gm_ref, gr_ref, gwi_hbm, gwo_hbm,
    normed, gu_all, go, sem, out_sem,
):
    gives = [
        pltpu.make_async_copy(gwo_made, gwo_hbm.at[0], out_sem.at[0]),
        pltpu.make_async_copy(gwi_made, gwi_hbm.at[0], out_sem.at[1]),
    ]
    loads = [
        pltpu.make_async_copy(src, dst, sem.at[i])
        for i, (src, dst) in enumerate(((gu_hbm, gu_all), (norm_hbm, normed), (go_hbm, go)))
    ]
    for copy in loads + gives:
        copy.start()
    for j in range(8):
        gr_ref[:, j * 128 : (j + 1) * 128] = col_ref[:, j, :]
    for load in loads:
        load.wait()

    scale = 1.0 + mod_ref[0, 1:2, :].astype(F32)
    mean_n = jnp.zeros((TOK, 1), F32)
    slope_n = jnp.zeros((TOK, 1), F32)
    for part in range(2):
        at = slice(part * HALF, (part + 1) * HALF)
        gu = gu_all[part * TOK : (part + 1) * TOK, :]
        gn_n = gu * normed[:, at]
        gm_ref[0, 0:1, at] = jnp.sum(gu, axis=0, keepdims=True)
        gm_ref[0, 1:2, at] = jnp.sum(gn_n, axis=0, keepdims=True)
        mean_n += jnp.sum(gu * scale[:, at], axis=1, keepdims=True)
        slope_n += jnp.sum(gn_n * scale[:, at], axis=1, keepdims=True)
    mean_n = mean_n * (1.0 / WIDTH)
    slope_n = slope_n * (1.0 / WIDTH)
    inv_t = inverse[:, 0:1]
    for part in range(2):
        at = slice(part * HALF, (part + 1) * HALF)
        gu = gu_all[part * TOK : (part + 1) * TOK, :]
        gt_ref[:, at] = (
            go[:, at].astype(F32)
            + (gu * scale[:, at] - mean_n - normed[:, at] * slope_n) * inv_t
        ).astype(BF16)
    for give in gives:
        give.wait()


def body(tokens, modulation, router_weight, weight_in, weight_out, chosen, grad_out):
    vmem = pl.BlockSpec(memory_space=pltpu.VMEM)
    hbm = pl.BlockSpec(memory_space=pl.ANY)
    sds = jax.ShapeDtypeStruct
    slots = pltpu.VMEM((SLOTS, HALF), BF16)
    rows = pltpu.VMEM((2 * CAP, WIDTH), BF16)
    inner = pltpu.VMEM((2 * CAP, HIDL), BF16)
    column = pltpu.VMEM((8, 128), F32)
    thin = pltpu.VMEM((2 * CAP, 128), F32)
    gwo, gwi, normed, inverse, gu, columns = pl.pallas_call(
        kernel,
        out_shape=(
            sds((HIDL, WIDTH), BF16),
            sds((WIDTH, HIDL), BF16),
            sds((TOK, WIDTH), F32),
            sds((TOK, 128), F32),
            sds((2 * TOK, HALF), F32),
            sds((EXPERTS * 8, 128), F32),
        ),
        in_specs=[vmem, vmem, vmem, hbm, hbm, vmem, vmem],
        out_specs=(vmem, vmem, hbm, vmem, vmem, vmem),
        scratch_shapes=[
            pltpu.VMEM((WIDTH, HIDL), BF16),
            pltpu.VMEM((HIDL, WIDTH), BF16),
            pltpu.VMEM((SLOTS, 2 * TOK), BF16),
            pltpu.VMEM((2 * CAP, SLOTS), BF16),
            pltpu.VMEM((SLOTS, 2 * CAP), BF16),
            pltpu.VMEM((SLOTS, 2 * CAP), BF16),
            slots, slots, slots, slots,
            rows, rows, rows,
            pltpu.VMEM((2 * CAP, HIDL), F32),
            inner, inner,
            pltpu.VMEM((2 * CAP, HALF), BF16),
            slots, slots, slots, slots,
            pltpu.VMEM((2 * TOK, HALF), BF16),
            pltpu.VMEM((TOK, WIDTH), F32),
            thin, thin, thin,
            column, column, column,
            pltpu.VMEM((EXPERTS * 8, 128), F32),
            pltpu.VMEM((8, WIDTH), F32),
            pltpu.VMEM((8, CAP), jnp.int32),
            pltpu.VMEM((8, CAP), jnp.int32),
            pltpu.SemaphoreType.DMA((2,)),
            pltpu.SemaphoreType.DMA((5,)),
            pltpu.SemaphoreType.DMA((5,)),
            pltpu.SemaphoreType.DMA((5,)),
            pltpu.SemaphoreType.DMA((4,)),
            pltpu.SemaphoreType.DMA((4,)),
        ],
        compiler_params=pltpu.CompilerParams(collective_id=0, has_side_effects=True, vmem_limit_bytes=40 * 2**20),
    )(tokens, modulation, router_weight.T, weight_in, weight_out, chosen, grad_out)
    grad_tokens, grad_mod, columns, grad_weight_in, grad_weight_out = pl.pallas_call(
        finish,
        out_shape=(
            sds((TOK, WIDTH), BF16),
            sds((1, 2, WIDTH), F32),
            sds((EXPERTS, WIDTH), F32),
            sds((1, WIDTH, HIDL), BF16),
            sds((1, HIDL, WIDTH), BF16),
        ),
        in_specs=[hbm] * 5 + [vmem] * 3,
        out_specs=(vmem, vmem, vmem, hbm, hbm),
        scratch_shapes=[
            pltpu.VMEM((TOK, WIDTH), F32),
            pltpu.VMEM((2 * TOK, HALF), F32),
            pltpu.VMEM((TOK, WIDTH), BF16),
            pltpu.SemaphoreType.DMA((3,)),
            pltpu.SemaphoreType.DMA((2,)),
        ],
        compiler_params=pltpu.CompilerParams(vmem_limit_bytes=16 * 2**20),
    )(
        gwo, gwi, normed, gu, grad_out, inverse, modulation,
        columns.reshape(EXPERTS, 8, 128),
    )
    return (grad_tokens, grad_mod, columns.T, grad_weight_in, grad_weight_out)


def solution(mesh):
    placed = (
        P(("dp", "expert"), None),
        P(("dp", "expert"), None, None),
        P(),
        P("expert", None, "dp"),
        P("expert", "dp", None),
        P("dp", None, None),
        P(("dp", "expert"), None),
    )
    return jax.shard_map(
        body,
        mesh=mesh,
        in_specs=placed,
        out_specs=(
            P(("dp", "expert"), None),
            P(("dp", "expert"), None, None),
            P(),
            P("expert", None, "dp"),
            P("expert", "dp", None),
        ),
        check_vma=False,
    )
```

```python
import jax
import jax.numpy as jnp
from jax import lax
from jax.experimental import pallas as pl
from jax.experimental.pallas import tpu as pltpu
from jax.sharding import PartitionSpec as P

gelu_root = 0.7978845608028654
gelu_cube = 0.044715
norm_eps = 1e-06

TOK = 256
WIDTH = 1024
HALF = 512
HIDL = 2048
EXPERTS = 64
CAP = 256
SLOTS = EXPERTS * 16
TILE = 256
STEP = 21
STEP_INV = 61
F32 = jnp.float32
BF16 = jnp.bfloat16
MESH = pl.DeviceIdType.MESH


def iota(shape, dim):
    return lax.broadcasted_iota(jnp.int32, shape, dim)


def dot(a, b):
    return jnp.dot(a, b, preferred_element_type=F32)


def dot_nt(a, b):
    return lax.dot_general(a, b, (((1,), (1,)), ((), ())), preferred_element_type=F32)


def dot_tn(a, b):
    return lax.dot_general(a, b, (((0,), (0,)), ((), ())), preferred_element_type=F32)


def kernel(
    tok_ref, mod_ref, rw_ref, w_in_hbm, w_out_hbm, chosen_ref, go_ref,
    stage, stage_in, norm_hbm, inverse, gu_ref, col_out,
    w_in, w_out, sel, sel_t, comp, comp_t, comp_p,
    g_send, u_send, g_recv, u_recv, g_all, u_all, gy_all,
    up_scr, hid, gp, parts, ret_send, ret_recv, pret_send, pret_recv,
    halves, normed, scores, q_all, logit, col_mine, col_theirs, col_sum, col_recv, rw_row, list_mine, list_theirs,
    w_sem, out_sem, send_sem, recv_sem, pair_send, pair_recv,
):
    d = lax.axis_index("dp")
    me = lax.axis_index("expert")
    other = 1 - d

    load_out = pltpu.make_async_copy(w_out_hbm.at[0], w_out, w_sem.at[0])
    load_in = pltpu.make_async_copy(w_in_hbm.at[0], w_in, w_sem.at[1])
    load_out.start()
    load_in.start()

    barrier = pltpu.get_barrier_semaphore()

    def greet(step, carry):
        peer = (me + step) & (EXPERTS - 1)
        pl.semaphore_signal(barrier, inc=1, device_id=(d, peer), device_id_type=MESH)
        pl.semaphore_signal(barrier, inc=1, device_id=(other, peer), device_id_type=MESH)
        return carry

    pl.semaphore_signal(barrier, inc=1, device_id=(other, me), device_id_type=MESH)
    lax.fori_loop(1, EXPERTS, greet, 0)

    local = chosen_ref[0] - me * TOK
    mine = (local >= 0) & (local < TOK)
    before = jnp.where(iota((CAP, CAP), 0) < iota((CAP, CAP), 1), 1.0, 0.0).astype(BF16)
    rank = dot(jnp.where(mine, 1.0, 0.0).astype(BF16), before)
    local_f = (local + 1).astype(F32)
    lane = iota((EXPERTS, 128), 1)
    values = jnp.zeros((EXPERTS, 128), F32)
    for k in range(8):
        one = jnp.sum(
            jnp.where(mine & (rank == float(k)), local_f, 0.0), axis=1, keepdims=True
        )
        values = jnp.where(lane == k, one, values)
    values = values.astype(BF16)

    def fill_sel(i, carry):
        rows = pl.multiple_of(i * TILE, TILE)
        row = rows + iota((TILE, EXPERTS), 0)
        expert = ((row >> 4) * STEP + me) & (EXPERTS - 1)
        spread = dot(jnp.where(expert == iota((TILE, EXPERTS), 1), 1.0, 0.0).astype(BF16), values)
        row_k = iota((TILE, 128), 0) & 7
        token = jnp.sum(
            jnp.where(row_k == iota((TILE, 128), 1), spread, 0.0), axis=1, keepdims=True
        )
        part = ((iota((TILE, 1), 0) >> 3) & 1).astype(F32) * float(TOK)
        target = jnp.where(token > 0.5, token - 1.0 + part, -1.0)
        sel[pl.ds(rows, TILE), :] = jnp.where(
            iota((TILE, 2 * TOK), 1).astype(F32) == target, 1.0, 0.0
        ).astype(BF16)
        return carry

    lax.fori_loop(0, SLOTS // TILE, fill_sel, 0)

    def spread_rows(out):
        def step(i, carry):
            rows = pl.multiple_of(i * TILE, TILE)
            out[pl.ds(rows, TILE), :] = dot(sel[pl.ds(rows, TILE), :], halves[...]).astype(BF16)
            return carry

        lax.fori_loop(0, SLOTS // TILE, step, 0)

    def send_all(src, dst, which, sign, size, to, first, last=EXPERTS):
        def step(i, carry):
            rows = pl.ds(pl.multiple_of(i * size, size), size)
            pltpu.make_async_remote_copy(
                src_ref=src.at[rows],
                dst_ref=dst.at[rows],
                send_sem=send_sem.at[which],
                recv_sem=recv_sem.at[which],
                device_id=(to, (me + (sign * STEP) % EXPERTS * i) & (EXPERTS - 1)),
                device_id_type=MESH,
            ).start()
            return carry

        lax.fori_loop(first, last, step, 0)

    def all_of(src, dst, which, size, first):
        rows = pl.ds(first * size, (EXPERTS - first) * size)
        return pltpu.make_async_remote_copy(
            src_ref=src.at[rows],
            dst_ref=dst.at[rows],
            send_sem=send_sem.at[which],
            recv_sem=recv_sem.at[which],
            device_id=(d, (me + 1) & (EXPERTS - 1)),
            device_id_type=MESH,
        )

    def keep(src, dst, which):
        return pltpu.make_async_copy(src, dst, out_sem.at[which])

    def to_partner(src, dst, which):
        return pltpu.make_async_remote_copy(
            src_ref=src,
            dst_ref=dst,
            send_sem=pair_send.at[which],
            recv_sem=pair_recv.at[which],
            device_id=(other, me),
            device_id_type=MESH,
        )

    halves[0:TOK, :] = go_ref[:, 0:HALF]
    halves[TOK:, :] = go_ref[:, HALF:]
    spread_rows(g_send)
    pl.semaphore_wait(barrier, 2 * EXPERTS - 1)
    send_all(g_send, g_recv, 0, 1, 16, d, 1)
    one_row = chosen_ref[0, pl.ds(me, 1), :]
    list_mine[...] = jnp.broadcast_to(one_row, (8, CAP))
    to_partner(list_mine, list_theirs, 2).start()
    g_recv[0:16, :] = g_send[0:16, :]

    shift = mod_ref[0, 0:1, :].astype(F32)
    scale = 1.0 + mod_ref[0, 1:2, :].astype(F32)
    x = tok_ref[...].astype(F32)
    centred = x - jnp.mean(x, axis=1, keepdims=True)
    inv = lax.rsqrt(jnp.mean(centred * centred, axis=1, keepdims=True) + norm_eps)
    nrm = centred * inv
    normed[...] = nrm
    keep(normed, norm_hbm, 0).start()
    inverse[...] = jnp.broadcast_to(inv, (TOK, 128))
    u = (nrm * scale + shift).astype(BF16)
    halves[0:TOK, :] = u[:, 0:HALF]
    halves[TOK:, :] = u[:, HALF:]
    spread_rows(u_send)
    send_all(u_send, u_recv, 1, 1, 16, d, 1)
    u_recv[0:16, :] = u_send[0:16, :]

    r_i, c_i = iota((CAP, CAP), 0), iota((CAP, CAP), 1)

    def places(row):
        img_row = row >> 8
        img_col = jnp.sum(jnp.where(r_i == c_i, img_row, 0), axis=1, keepdims=True)
        same = img_col == img_row
        rank_row = jnp.sum(jnp.where(same & (r_i < c_i), 1, 0), axis=0, keepdims=True)
        slot_row = (((me - img_row + EXPERTS) * STEP_INV) & (EXPERTS - 1)) * 16 + rank_row
        return img_col, same, slot_row

    def fill_back(slot_row, out):
        for part in range(2):
            out[:, part * CAP : (part + 1) * CAP] = jnp.where(
                iota((SLOTS, CAP), 0) == slot_row + 8 * part, 1.0, 0.0
            ).astype(BF16)

    img_col, same, slot_row = places(one_row)
    rank_col = jnp.sum(jnp.where(same & (c_i < r_i), 1, 0), axis=1, keepdims=True)
    slot_col = (((me - img_col + EXPERTS) * STEP_INV) & (EXPERTS - 1)) * 16 + rank_col
    for part in range(2):
        comp[part * CAP : (part + 1) * CAP, :] = jnp.where(
            iota((CAP, SLOTS), 1) == slot_col + 8 * part, 1.0, 0.0
        ).astype(BF16)
    fill_back(slot_row, comp_t)
    sel_t[...] = sel[...].T
    to_partner(list_mine, list_theirs, 2).wait()
    fill_back(places(list_theirs[0:1, :])[2], comp_p)

    pick = jnp.where(iota((16, EXPERTS), 1) == me, 1.0, 0.0).astype(BF16)
    rw_row[...] = dot(pick, rw_ref[...])[0:8]
    rw_e = rw_row[0:1, :]

    def compact(recv, out):
        for part in range(2):
            out[0:CAP, part * HALF : (part + 1) * HALF] = dot(
                comp[part * CAP : (part + 1) * CAP, :], recv[...]
            ).astype(BF16)

    def upstream(s):
        rows = slice(s * CAP, (s + 1) * CAP)

        def step(n, carry):
            cols = pl.ds(pl.multiple_of(n * TILE, TILE), TILE)
            up_scr[rows, cols] = dot_nt(g_all[rows, :], w_out[cols, :])
            return carry

        lax.fori_loop(0, HIDL // TILE, step, 0, unroll=4)

    def gates(s):
        rows = slice(s * CAP, (s + 1) * CAP)
        logits = jnp.sum(u_all[rows, :].astype(F32) * rw_e, axis=1, keepdims=True)
        q = jax.nn.sigmoid(logits).astype(BF16).astype(F32)
        q_all[rows, :] = jnp.broadcast_to(q, (CAP, 128))

    def weigh(s):
        rows = slice(s * CAP, (s + 1) * CAP)
        gy_all[rows, :] = (q_all[rows, 0:1] * g_all[rows, :].astype(F32)).astype(BF16)

    def middle(s):
        rows = slice(s * CAP, (s + 1) * CAP)
        q = q_all[rows, 0:1]
        scores[rows, :] = jnp.zeros((CAP, 128), F32)

        def step(n, carry):
            cols = pl.ds(pl.multiple_of(n * TILE, TILE), TILE)
            a = dot(u_all[rows, :], w_in[:, cols])
            up = up_scr[rows, cols]
            a2 = a * a
            t = jnp.tanh(gelu_root * a * (1.0 + gelu_cube * a2))
            half = 0.5 * (1.0 + t)
            h = (a * half).astype(BF16)
            slope = half + (0.5 * gelu_root) * a * (1.0 - t * t) * (1.0 + (3.0 * gelu_cube) * a2)
            hid[rows, cols] = h
            gp[rows, cols] = (q * up * slope).astype(BF16)
            prod = h.astype(F32) * up
            scores[rows, :] += prod[:, 0:128] + prod[:, 128:256]
            return carry

        lax.fori_loop(0, HIDL // TILE, step, 0, unroll=4)
        score = jnp.sum(scores[rows, :], axis=1, keepdims=True)
        logit[rows, :] = jnp.broadcast_to(score * q * (1.0 - q), (CAP, 128))

    def row_gradients(s, places_t, send, recv, which, to, first):
        rows = slice(s * CAP, (s + 1) * CAP)
        for part in range(2):
            at = slice(part * HALF, (part + 1) * HALF)
            parts[part * CAP : (part + 1) * CAP, :] = (
                dot_nt(gp[rows, :], w_in[at, :]) + logit[rows, 0:1] * rw_e[:, at]
            ).astype(BF16)

        def step(i, carry):
            slots = pl.ds(pl.multiple_of(i * TILE, TILE), TILE)
            send[slots, :] = dot(places_t[slots, :], parts[...]).astype(BF16)
            here = TILE // 16
            send_all(send, recv, which, -1, 16, to, jnp.maximum(i * here, first), (i + 1) * here)
            return carry

        lax.fori_loop(0, SLOTS // TILE, step, 0)

    all_of(g_send, g_recv, 0, 16, 1).wait_recv()
    compact(g_recv, g_all)
    to_partner(g_all.at[0:CAP], g_all.at[CAP:], 0).start()
    load_out.wait()
    upstream(0)

    all_of(u_send, u_recv, 1, 16, 1).wait_recv()
    compact(u_recv, u_all)
    to_partner(u_all.at[0:CAP], u_all.at[CAP:], 1).start()
    to_partner(g_all.at[0:CAP], g_all.at[CAP:], 0).wait()
    upstream(1)
    load_in.wait()
    gates(0)
    middle(0)
    row_gradients(0, comp_t, ret_send, ret_recv, 2, d, 1)
    ret_recv[0:16, :] = ret_send[0:16, :]

    to_partner(u_all.at[0:CAP], u_all.at[CAP:], 1).wait()
    gates(1)
    middle(1)
    row_gradients(1, comp_p, pret_send, pret_recv, 4, other, 0)
    weigh(0)
    weigh(1)

    column = jnp.sum(u_all[...].astype(F32) * logit[:, 0:1], axis=0, keepdims=True)
    for j in range(8):
        col_mine[j : j + 1, :] = column[:, j * 128 : (j + 1) * 128]
    to_partner(col_mine, col_theirs, 3).start()

    def grad_out_tile(n, carry):
        cols = pl.ds(pl.multiple_of(n * TILE, TILE), TILE)
        stage[cols, :] = dot_tn(hid[:, cols], gy_all[...]).astype(BF16)
        return carry

    lax.fori_loop(0, HIDL // TILE, grad_out_tile, 0)
    to_partner(col_mine, col_theirs, 3).wait()
    col_sum[...] = col_mine[...] + col_theirs[...]

    def share_column(i, carry):
        pltpu.make_async_remote_copy(
            src_ref=col_sum,
            dst_ref=col_recv.at[pl.ds(pl.multiple_of(me * 8, 8), 8)],
            send_sem=send_sem.at[3],
            recv_sem=recv_sem.at[3],
            device_id=(d, (me + STEP * i) & (EXPERTS - 1)),
            device_id_type=MESH,
        ).start()
        return carry

    lax.fori_loop(1, EXPERTS, share_column, 0)

    def grad_in_tile(n, carry):
        cols = pl.ds(pl.multiple_of(n * TILE, TILE), TILE)
        stage_in[cols, :] = dot_tn(u_all[:, cols], gp[...]).astype(BF16)
        return carry

    lax.fori_loop(0, WIDTH // TILE, grad_in_tile, 0)
    all_of(g_send, g_recv, 0, 16, 1).wait_send()
    all_of(u_send, u_recv, 1, 16, 1).wait_send()

    def gather_back(recv, first):
        for part in range(2):
            rows = slice(part * TOK, (part + 1) * TOK)
            back = dot(sel_t[rows, :], recv[...])
            gu_ref[rows, :] = back if first else gu_ref[rows, :] + back

    all_of(ret_send, ret_recv, 2, 16, 1).wait()
    gather_back(ret_recv, True)
    column_wait = all_of(col_recv, col_recv, 3, 8, 1)
    column_wait.wait_recv()
    column_wait.wait_send()
    col_recv[pl.ds(pl.multiple_of(me * 8, 8), 8), :] = col_sum[...]
    col_out[...] = col_recv[...]
    all_of(pret_send, pret_recv, 4, 16, 0).wait()
    gather_back(pret_recv, False)
    keep(normed, norm_hbm, 0).wait()


def finish(
    gwo_made, gwi_made, normed, gu_all, go, inverse, mod_ref, col_ref,
    gt_ref, gm_ref, gr_ref, gwi_hbm, gwo_hbm,
    out_sem,
):
    gives = [
        pltpu.make_async_copy(gwo_made, gwo_hbm.at[0], out_sem.at[0]),
        pltpu.make_async_copy(gwi_made, gwi_hbm.at[0], out_sem.at[1]),
    ]
    for give in gives:
        give.start()
    for j in range(8):
        gr_ref[:, j * 128 : (j + 1) * 128] = col_ref[:, j, :]
    scale = 1.0 + mod_ref[0, 1:2, :].astype(F32)
    mean_n = jnp.zeros((TOK, 1), F32)
    slope_n = jnp.zeros((TOK, 1), F32)
    for part in range(2):
        at = slice(part * HALF, (part + 1) * HALF)
        gu = gu_all[part * TOK : (part + 1) * TOK, :]
        gn_n = gu * normed[:, at]
        gm_ref[0, 0:1, at] = jnp.sum(gu, axis=0, keepdims=True)
        gm_ref[0, 1:2, at] = jnp.sum(gn_n, axis=0, keepdims=True)
        mean_n += jnp.sum(gu * scale[:, at], axis=1, keepdims=True)
        slope_n += jnp.sum(gn_n * scale[:, at], axis=1, keepdims=True)
    mean_n = mean_n * (1.0 / WIDTH)
    slope_n = slope_n * (1.0 / WIDTH)
    inv_t = inverse[:, 0:1]
    for part in range(2):
        at = slice(part * HALF, (part + 1) * HALF)
        gu = gu_all[part * TOK : (part + 1) * TOK, :]
        gt_ref[:, at] = (
            go[:, at].astype(F32)
            + (gu * scale[:, at] - mean_n - normed[:, at] * slope_n) * inv_t
        ).astype(BF16)
    for give in gives:
        give.wait()


def body(tokens, modulation, router_weight, weight_in, weight_out, chosen, grad_out):
    vmem = pl.BlockSpec(memory_space=pltpu.VMEM)
    hbm = pl.BlockSpec(memory_space=pl.ANY)
    sds = jax.ShapeDtypeStruct
    slots = pltpu.VMEM((SLOTS, HALF), BF16)
    rows = pltpu.VMEM((2 * CAP, WIDTH), BF16)
    inner = pltpu.VMEM((2 * CAP, HIDL), BF16)
    column = pltpu.VMEM((8, 128), F32)
    thin = pltpu.VMEM((2 * CAP, 128), F32)
    gwo, gwi, normed, inverse, gu, columns = pl.pallas_call(
        kernel,
        out_shape=(
            sds((HIDL, WIDTH), BF16),
            sds((WIDTH, HIDL), BF16),
            sds((TOK, WIDTH), F32),
            sds((TOK, 128), F32),
            sds((2 * TOK, HALF), F32),
            sds((EXPERTS * 8, 128), F32),
        ),
        in_specs=[vmem, vmem, vmem, hbm, hbm, vmem, vmem],
        out_specs=(vmem, vmem, hbm, vmem, vmem, vmem),
        scratch_shapes=[
            pltpu.VMEM((WIDTH, HIDL), BF16),
            pltpu.VMEM((HIDL, WIDTH), BF16),
            pltpu.VMEM((SLOTS, 2 * TOK), BF16),
            pltpu.VMEM((2 * TOK, SLOTS), BF16),
            pltpu.VMEM((2 * CAP, SLOTS), BF16),
            pltpu.VMEM((SLOTS, 2 * CAP), BF16),
            pltpu.VMEM((SLOTS, 2 * CAP), BF16),
            slots, slots, slots, slots,
            rows, rows, rows,
            pltpu.VMEM((2 * CAP, HIDL), F32),
            inner, inner,
            pltpu.VMEM((2 * CAP, HALF), BF16),
            slots, slots, slots, slots,
            pltpu.VMEM((2 * TOK, HALF), BF16),
            pltpu.VMEM((TOK, WIDTH), F32),
            thin, thin, thin,
            column, column, column,
            pltpu.VMEM((EXPERTS * 8, 128), F32),
            pltpu.VMEM((8, WIDTH), F32),
            pltpu.VMEM((8, CAP), jnp.int32),
            pltpu.VMEM((8, CAP), jnp.int32),
            pltpu.SemaphoreType.DMA((2,)),
            pltpu.SemaphoreType.DMA((5,)),
            pltpu.SemaphoreType.DMA((5,)),
            pltpu.SemaphoreType.DMA((5,)),
            pltpu.SemaphoreType.DMA((4,)),
            pltpu.SemaphoreType.DMA((4,)),
        ],
        compiler_params=pltpu.CompilerParams(collective_id=0, has_side_effects=True, vmem_limit_bytes=40 * 2**20),
    )(tokens, modulation, router_weight.T, weight_in, weight_out, chosen, grad_out)
    grad_tokens, grad_mod, columns, grad_weight_in, grad_weight_out = pl.pallas_call(
        finish,
        out_shape=(
            sds((TOK, WIDTH), BF16),
            sds((1, 2, WIDTH), F32),
            sds((EXPERTS, WIDTH), F32),
            sds((1, WIDTH, HIDL), BF16),
            sds((1, HIDL, WIDTH), BF16),
        ),
        in_specs=[hbm] * 2 + [vmem] * 6,
        out_specs=(vmem, vmem, vmem, hbm, hbm),
        scratch_shapes=[
            pltpu.SemaphoreType.DMA((2,)),
        ],
        compiler_params=pltpu.CompilerParams(vmem_limit_bytes=16 * 2**20),
    )(
        gwo, gwi, normed, gu, grad_out, inverse, modulation,
        columns.reshape(EXPERTS, 8, 128),
    )
    return (grad_tokens, grad_mod, columns.T, grad_weight_in, grad_weight_out)


def solution(mesh):
    placed = (
        P(("dp", "expert"), None),
        P(("dp", "expert"), None, None),
        P(),
        P("expert", None, "dp"),
        P("expert", "dp", None),
        P("dp", None, None),
        P(("dp", "expert"), None),
    )
    return jax.shard_map(
        body,
        mesh=mesh,
        in_specs=placed,
        out_specs=(
            P(("dp", "expert"), None),
            P(("dp", "expert"), None, None),
            P(),
            P("expert", None, "dp"),
            P("expert", "dp", None),
        ),
        check_vma=False,
    )
```

```python
import jax
import jax.numpy as jnp
from jax import lax
from jax.experimental import pallas as pl
from jax.experimental.pallas import tpu as pltpu
from jax.sharding import PartitionSpec as P

gelu_root = 0.7978845608028654
gelu_cube = 0.044715
norm_eps = 1e-06

TOK = 256
WIDTH = 1024
HALF = 512
HIDL = 2048
EXPERTS = 64
CAP = 256
SLOTS = EXPERTS * 16
TILE = 256
STEP = 21
STEP_INV = 61
F32 = jnp.float32
BF16 = jnp.bfloat16
MESH = pl.DeviceIdType.MESH


def iota(shape, dim):
    return lax.broadcasted_iota(jnp.int32, shape, dim)


def dot(a, b):
    return jnp.dot(a, b, preferred_element_type=F32)


def dot_nt(a, b):
    return lax.dot_general(a, b, (((1,), (1,)), ((), ())), preferred_element_type=F32)


def dot_tn(a, b):
    return lax.dot_general(a, b, (((0,), (0,)), ((), ())), preferred_element_type=F32)


def kernel(
    tok_ref, mod_ref, rw_ref, w_in_hbm, w_out_hbm, chosen_ref, go_ref,
    stage, stage_in, norm_hbm, inverse, gu_ref, col_out,
    w_in, w_out, sel, sel_t, comp, comp_t, comp_p,
    g_send, u_send, g_recv, u_recv, g_all, u_all, gy_all,
    up_scr, hid, gp, parts, ret_send, ret_recv, pret_send, pret_recv,
    halves, normed, scores, q_all, logit, col_mine, col_theirs, col_sum, col_recv, rw_row, list_mine, list_theirs,
    w_sem, out_sem, send_sem, recv_sem, pair_send, pair_recv,
):
    d = lax.axis_index("dp")
    me = lax.axis_index("expert")
    other = 1 - d

    load_out = pltpu.make_async_copy(w_out_hbm.at[0], w_out, w_sem.at[0])
    load_in = pltpu.make_async_copy(w_in_hbm.at[0], w_in, w_sem.at[1])
    load_out.start()
    load_in.start()

    barrier = pltpu.get_barrier_semaphore()

    def greet(step, carry):
        peer = (me + step) & (EXPERTS - 1)
        pl.semaphore_signal(barrier, inc=1, device_id=(d, peer), device_id_type=MESH)
        pl.semaphore_signal(barrier, inc=1, device_id=(other, peer), device_id_type=MESH)
        return carry

    pl.semaphore_signal(barrier, inc=1, device_id=(other, me), device_id_type=MESH)
    lax.fori_loop(1, EXPERTS, greet, 0)

    local = chosen_ref[0] - me * TOK
    mine = (local >= 0) & (local < TOK)
    before = jnp.where(iota((CAP, CAP), 0) < iota((CAP, CAP), 1), 1.0, 0.0).astype(BF16)
    rank = dot(jnp.where(mine, 1.0, 0.0).astype(BF16), before)
    local_f = (local + 1).astype(F32)
    lane = iota((EXPERTS, 128), 1)
    values = jnp.zeros((EXPERTS, 128), F32)
    for k in range(8):
        one = jnp.sum(
            jnp.where(mine & (rank == float(k)), local_f, 0.0), axis=1, keepdims=True
        )
        values = jnp.where(lane == k, one, values)
    values = values.astype(BF16)

    def fill_sel(i, carry):
        rows = pl.multiple_of(i * TILE, TILE)
        row = rows + iota((TILE, EXPERTS), 0)
        expert = ((row >> 4) * STEP + me) & (EXPERTS - 1)
        spread = dot(jnp.where(expert == iota((TILE, EXPERTS), 1), 1.0, 0.0).astype(BF16), values)
        row_k = iota((TILE, 128), 0) & 7
        token = jnp.sum(
            jnp.where(row_k == iota((TILE, 128), 1), spread, 0.0), axis=1, keepdims=True
        )
        part = ((iota((TILE, 1), 0) >> 3) & 1).astype(F32) * float(TOK)
        target = jnp.where(token > 0.5, token - 1.0 + part, -1.0)
        sel[pl.ds(rows, TILE), :] = jnp.where(
            iota((TILE, 2 * TOK), 1).astype(F32) == target, 1.0, 0.0
        ).astype(BF16)
        return carry

    lax.fori_loop(0, SLOTS // TILE, fill_sel, 0)

    def spread_rows(out):
        def step(i, carry):
            rows = pl.multiple_of(i * TILE, TILE)
            out[pl.ds(rows, TILE), :] = dot(sel[pl.ds(rows, TILE), :], halves[...]).astype(BF16)
            return carry

        lax.fori_loop(0, SLOTS // TILE, step, 0)

    def send_all(src, dst, which, sign, size, to, first, last=EXPERTS):
        def step(i, carry):
            rows = pl.ds(pl.multiple_of(i * size, size), size)
            pltpu.make_async_remote_copy(
                src_ref=src.at[rows],
                dst_ref=dst.at[rows],
                send_sem=send_sem.at[which],
                recv_sem=recv_sem.at[which],
                device_id=(to, (me + (sign * STEP) % EXPERTS * i) & (EXPERTS - 1)),
                device_id_type=MESH,
            ).start()
            return carry

        lax.fori_loop(first, last, step, 0)

    def all_of(src, dst, which, size, first):
        rows = pl.ds(first * size, (EXPERTS - first) * size)
        return pltpu.make_async_remote_copy(
            src_ref=src.at[rows],
            dst_ref=dst.at[rows],
            send_sem=send_sem.at[which],
            recv_sem=recv_sem.at[which],
            device_id=(d, (me + 1) & (EXPERTS - 1)),
            device_id_type=MESH,
        )

    def keep(src, dst, which):
        return pltpu.make_async_copy(src, dst, out_sem.at[which])

    def to_partner(src, dst, which):
        return pltpu.make_async_remote_copy(
            src_ref=src,
            dst_ref=dst,
            send_sem=pair_send.at[which],
            recv_sem=pair_recv.at[which],
            device_id=(other, me),
            device_id_type=MESH,
        )

    halves[0:TOK, :] = go_ref[:, 0:HALF]
    halves[TOK:, :] = go_ref[:, HALF:]
    spread_rows(g_send)
    pl.semaphore_wait(barrier, 2 * EXPERTS - 1)
    send_all(g_send, g_recv, 0, 1, 16, d, 1)
    one_row = chosen_ref[0, pl.ds(me, 1), :]
    list_mine[...] = jnp.broadcast_to(one_row, (8, CAP))
    to_partner(list_mine, list_theirs, 2).start()
    g_recv[0:16, :] = g_send[0:16, :]

    shift = mod_ref[0, 0:1, :].astype(F32)
    scale = 1.0 + mod_ref[0, 1:2, :].astype(F32)
    x = tok_ref[...].astype(F32)
    centred = x - jnp.mean(x, axis=1, keepdims=True)
    inv = lax.rsqrt(jnp.mean(centred * centred, axis=1, keepdims=True) + norm_eps)
    nrm = centred * inv
    normed[...] = nrm
    keep(normed, norm_hbm, 0).start()
    inverse[...] = jnp.broadcast_to(inv, (TOK, 128))
    u = (nrm * scale + shift).astype(BF16)
    halves[0:TOK, :] = u[:, 0:HALF]
    halves[TOK:, :] = u[:, HALF:]
    spread_rows(u_send)
    send_all(u_send, u_recv, 1, 1, 16, d, 1)
    u_recv[0:16, :] = u_send[0:16, :]

    r_i, c_i = iota((CAP, CAP), 0), iota((CAP, CAP), 1)

    def places(row):
        img_row = row >> 8
        img_col = jnp.sum(jnp.where(r_i == c_i, img_row, 0), axis=1, keepdims=True)
        same = img_col == img_row
        rank_row = jnp.sum(jnp.where(same & (r_i < c_i), 1, 0), axis=0, keepdims=True)
        slot_row = (((me - img_row + EXPERTS) * STEP_INV) & (EXPERTS - 1)) * 16 + rank_row
        return img_col, same, slot_row

    def fill_back(slot_row, out):
        for part in range(2):
            out[:, part * CAP : (part + 1) * CAP] = jnp.where(
                iota((SLOTS, CAP), 0) == slot_row + 8 * part, 1.0, 0.0
            ).astype(BF16)

    img_col, same, slot_row = places(one_row)
    rank_col = jnp.sum(jnp.where(same & (c_i < r_i), 1, 0), axis=1, keepdims=True)
    slot_col = (((me - img_col + EXPERTS) * STEP_INV) & (EXPERTS - 1)) * 16 + rank_col
    for part in range(2):
        comp[part * CAP : (part + 1) * CAP, :] = jnp.where(
            iota((CAP, SLOTS), 1) == slot_col + 8 * part, 1.0, 0.0
        ).astype(BF16)
    fill_back(slot_row, comp_t)
    sel_t[...] = sel[...].T
    to_partner(list_mine, list_theirs, 2).wait()
    fill_back(places(list_theirs[0:1, :])[2], comp_p)

    pick = jnp.where(iota((16, EXPERTS), 1) == me, 1.0, 0.0).astype(BF16)
    rw_row[...] = dot(pick, rw_ref[...])[0:8]
    rw_e = rw_row[0:1, :]

    def compact(recv, out):
        for part in range(2):
            out[0:CAP, part * HALF : (part + 1) * HALF] = dot(
                comp[part * CAP : (part + 1) * CAP, :], recv[...]
            ).astype(BF16)

    def upstream(s):
        rows = slice(s * CAP, (s + 1) * CAP)

        def step(n, carry):
            cols = pl.ds(pl.multiple_of(n * TILE, TILE), TILE)
            up_scr[rows, cols] = dot_nt(g_all[rows, :], w_out[cols, :])
            return carry

        lax.fori_loop(0, HIDL // TILE, step, 0, unroll=4)

    def gates(s):
        rows = slice(s * CAP, (s + 1) * CAP)
        logits = jnp.sum(u_all[rows, :].astype(F32) * rw_e, axis=1, keepdims=True)
        q = jax.nn.sigmoid(logits).astype(BF16).astype(F32)
        q_all[rows, :] = jnp.broadcast_to(q, (CAP, 128))

    def weigh(s):
        rows = slice(s * CAP, (s + 1) * CAP)
        gy_all[rows, :] = (q_all[rows, 0:1] * g_all[rows, :].astype(F32)).astype(BF16)

    def middle(s):
        rows = slice(s * CAP, (s + 1) * CAP)
        q = q_all[rows, 0:1]
        scores[rows, :] = jnp.zeros((CAP, 128), F32)

        def step(n, carry):
            cols = pl.ds(pl.multiple_of(n * TILE, TILE), TILE)
            a = dot(u_all[rows, :], w_in[:, cols])
            up = up_scr[rows, cols]
            a2 = a * a
            t = jnp.tanh(gelu_root * a * (1.0 + gelu_cube * a2))
            half = 0.5 * (1.0 + t)
            h = (a * half).astype(BF16)
            slope = half + (0.5 * gelu_root) * a * (1.0 - t * t) * (1.0 + (3.0 * gelu_cube) * a2)
            hid[rows, cols] = h
            gp[rows, cols] = (q * up * slope).astype(BF16)
            prod = h.astype(F32) * up
            scores[rows, :] += prod[:, 0:128] + prod[:, 128:256]
            return carry

        lax.fori_loop(0, HIDL // TILE, step, 0, unroll=4)
        score = jnp.sum(scores[rows, :], axis=1, keepdims=True)
        logit[rows, :] = jnp.broadcast_to(score * q * (1.0 - q), (CAP, 128))

    def row_gradients(s, places_t, send, recv, which, to, first):
        rows = slice(s * CAP, (s + 1) * CAP)
        for part in range(2):
            at = slice(part * HALF, (part + 1) * HALF)
            parts[part * CAP : (part + 1) * CAP, :] = (
                dot_nt(gp[rows, :], w_in[at, :]) + logit[rows, 0:1] * rw_e[:, at]
            ).astype(BF16)

        def step(i, carry):
            slots = pl.ds(pl.multiple_of(i * TILE, TILE), TILE)
            send[slots, :] = dot(places_t[slots, :], parts[...]).astype(BF16)
            here = TILE // 16
            send_all(send, recv, which, -1, 16, to, jnp.maximum(i * here, first), (i + 1) * here)
            return carry

        lax.fori_loop(0, SLOTS // TILE, step, 0)

    all_of(g_send, g_recv, 0, 16, 1).wait_recv()
    compact(g_recv, g_all)
    to_partner(g_all.at[0:CAP], g_all.at[CAP:], 0).start()
    load_out.wait()
    upstream(0)

    all_of(u_send, u_recv, 1, 16, 1).wait_recv()
    compact(u_recv, u_all)
    to_partner(u_all.at[0:CAP], u_all.at[CAP:], 1).start()
    to_partner(g_all.at[0:CAP], g_all.at[CAP:], 0).wait()
    upstream(1)
    load_in.wait()
    gates(0)
    middle(0)
    row_gradients(0, comp_t, ret_send, ret_recv, 2, d, 1)
    ret_recv[0:16, :] = ret_send[0:16, :]

    to_partner(u_all.at[0:CAP], u_all.at[CAP:], 1).wait()
    gates(1)
    middle(1)
    column = jnp.sum(u_all[...].astype(F32) * logit[:, 0:1], axis=0, keepdims=True)
    for j in range(8):
        col_mine[j : j + 1, :] = column[:, j * 128 : (j + 1) * 128]
    to_partner(col_mine, col_theirs, 3).start()

    row_gradients(1, comp_p, pret_send, pret_recv, 4, other, 0)
    to_partner(col_mine, col_theirs, 3).wait()
    col_sum[...] = col_mine[...] + col_theirs[...]

    def share_column(i, carry):
        pltpu.make_async_remote_copy(
            src_ref=col_sum,
            dst_ref=col_recv.at[pl.ds(pl.multiple_of(me * 8, 8), 8)],
            send_sem=send_sem.at[3],
            recv_sem=recv_sem.at[3],
            device_id=(d, (me + STEP * i) & (EXPERTS - 1)),
            device_id_type=MESH,
        ).start()
        return carry

    lax.fori_loop(1, EXPERTS, share_column, 0)
    weigh(0)
    weigh(1)

    def grad_out_tile(n, carry):
        cols = pl.ds(pl.multiple_of(n * TILE, TILE), TILE)
        stage[cols, :] = dot_tn(hid[:, cols], gy_all[...]).astype(BF16)
        return carry

    lax.fori_loop(0, HIDL // TILE, grad_out_tile, 0)

    def grad_in_tile(n, carry):
        cols = pl.ds(pl.multiple_of(n * TILE, TILE), TILE)
        stage_in[cols, :] = dot_tn(u_all[:, cols], gp[...]).astype(BF16)
        return carry

    lax.fori_loop(0, WIDTH // TILE, grad_in_tile, 0)
    all_of(g_send, g_recv, 0, 16, 1).wait_send()
    all_of(u_send, u_recv, 1, 16, 1).wait_send()

    def gather_back(recv, first):
        for part in range(2):
            rows = slice(part * TOK, (part + 1) * TOK)
            back = dot(sel_t[rows, :], recv[...])
            gu_ref[rows, :] = back if first else gu_ref[rows, :] + back

    all_of(ret_send, ret_recv, 2, 16, 1).wait()
    gather_back(ret_recv, True)
    all_of(pret_send, pret_recv, 4, 16, 0).wait()
    gather_back(pret_recv, False)
    column_wait = all_of(col_recv, col_recv, 3, 8, 1)
    column_wait.wait_recv()
    column_wait.wait_send()
    col_recv[pl.ds(pl.multiple_of(me * 8, 8), 8), :] = col_sum[...]
    col_out[...] = col_recv[...]
    keep(normed, norm_hbm, 0).wait()


def finish(
    gwo_made, gwi_made, normed, gu_all, go, inverse, mod_ref, col_ref,
    gt_ref, gm_ref, gr_ref, gwi_hbm, gwo_hbm,
    out_sem,
):
    gives = [
        pltpu.make_async_copy(gwo_made, gwo_hbm.at[0], out_sem.at[0]),
        pltpu.make_async_copy(gwi_made, gwi_hbm.at[0], out_sem.at[1]),
    ]
    for give in gives:
        give.start()
    for j in range(8):
        gr_ref[:, j * 128 : (j + 1) * 128] = col_ref[:, j, :]
    scale = 1.0 + mod_ref[0, 1:2, :].astype(F32)
    mean_n = jnp.zeros((TOK, 1), F32)
    slope_n = jnp.zeros((TOK, 1), F32)
    for part in range(2):
        at = slice(part * HALF, (part + 1) * HALF)
        gu = gu_all[part * TOK : (part + 1) * TOK, :]
        gn_n = gu * normed[:, at]
        gm_ref[0, 0:1, at] = jnp.sum(gu, axis=0, keepdims=True)
        gm_ref[0, 1:2, at] = jnp.sum(gn_n, axis=0, keepdims=True)
        mean_n += jnp.sum(gu * scale[:, at], axis=1, keepdims=True)
        slope_n += jnp.sum(gn_n * scale[:, at], axis=1, keepdims=True)
    mean_n = mean_n * (1.0 / WIDTH)
    slope_n = slope_n * (1.0 / WIDTH)
    inv_t = inverse[:, 0:1]
    for part in range(2):
        at = slice(part * HALF, (part + 1) * HALF)
        gu = gu_all[part * TOK : (part + 1) * TOK, :]
        gt_ref[:, at] = (
            go[:, at].astype(F32)
            + (gu * scale[:, at] - mean_n - normed[:, at] * slope_n) * inv_t
        ).astype(BF16)
    for give in gives:
        give.wait()


def body(tokens, modulation, router_weight, weight_in, weight_out, chosen, grad_out):
    vmem = pl.BlockSpec(memory_space=pltpu.VMEM)
    hbm = pl.BlockSpec(memory_space=pl.ANY)
    sds = jax.ShapeDtypeStruct
    slots = pltpu.VMEM((SLOTS, HALF), BF16)
    rows = pltpu.VMEM((2 * CAP, WIDTH), BF16)
    inner = pltpu.VMEM((2 * CAP, HIDL), BF16)
    column = pltpu.VMEM((8, 128), F32)
    thin = pltpu.VMEM((2 * CAP, 128), F32)
    gwo, gwi, normed, inverse, gu, columns = pl.pallas_call(
        kernel,
        out_shape=(
            sds((HIDL, WIDTH), BF16),
            sds((WIDTH, HIDL), BF16),
            sds((TOK, WIDTH), F32),
            sds((TOK, 128), F32),
            sds((2 * TOK, HALF), F32),
            sds((EXPERTS * 8, 128), F32),
        ),
        in_specs=[vmem, vmem, vmem, hbm, hbm, vmem, vmem],
        out_specs=(vmem, vmem, hbm, vmem, vmem, vmem),
        scratch_shapes=[
            pltpu.VMEM((WIDTH, HIDL), BF16),
            pltpu.VMEM((HIDL, WIDTH), BF16),
            pltpu.VMEM((SLOTS, 2 * TOK), BF16),
            pltpu.VMEM((2 * TOK, SLOTS), BF16),
            pltpu.VMEM((2 * CAP, SLOTS), BF16),
            pltpu.VMEM((SLOTS, 2 * CAP), BF16),
            pltpu.VMEM((SLOTS, 2 * CAP), BF16),
            slots, slots, slots, slots,
            rows, rows, rows,
            pltpu.VMEM((2 * CAP, HIDL), F32),
            inner, inner,
            pltpu.VMEM((2 * CAP, HALF), BF16),
            slots, slots, slots, slots,
            pltpu.VMEM((2 * TOK, HALF), BF16),
            pltpu.VMEM((TOK, WIDTH), F32),
            thin, thin, thin,
            column, column, column,
            pltpu.VMEM((EXPERTS * 8, 128), F32),
            pltpu.VMEM((8, WIDTH), F32),
            pltpu.VMEM((8, CAP), jnp.int32),
            pltpu.VMEM((8, CAP), jnp.int32),
            pltpu.SemaphoreType.DMA((2,)),
            pltpu.SemaphoreType.DMA((5,)),
            pltpu.SemaphoreType.DMA((5,)),
            pltpu.SemaphoreType.DMA((5,)),
            pltpu.SemaphoreType.DMA((4,)),
            pltpu.SemaphoreType.DMA((4,)),
        ],
        compiler_params=pltpu.CompilerParams(collective_id=0, has_side_effects=True, vmem_limit_bytes=40 * 2**20),
    )(tokens, modulation, router_weight.T, weight_in, weight_out, chosen, grad_out)
    grad_tokens, grad_mod, columns, grad_weight_in, grad_weight_out = pl.pallas_call(
        finish,
        out_shape=(
            sds((TOK, WIDTH), BF16),
            sds((1, 2, WIDTH), F32),
            sds((EXPERTS, WIDTH), F32),
            sds((1, WIDTH, HIDL), BF16),
            sds((1, HIDL, WIDTH), BF16),
        ),
        in_specs=[hbm] * 2 + [vmem] * 6,
        out_specs=(vmem, vmem, vmem, hbm, hbm),
        scratch_shapes=[
            pltpu.SemaphoreType.DMA((2,)),
        ],
        compiler_params=pltpu.CompilerParams(vmem_limit_bytes=16 * 2**20),
    )(
        gwo, gwi, normed, gu, grad_out, inverse, modulation,
        columns.reshape(EXPERTS, 8, 128),
    )
    return (grad_tokens, grad_mod, columns.T, grad_weight_in, grad_weight_out)


def solution(mesh):
    placed = (
        P(("dp", "expert"), None),
        P(("dp", "expert"), None, None),
        P(),
        P("expert", None, "dp"),
        P("expert", "dp", None),
        P("dp", None, None),
        P(("dp", "expert"), None),
    )
    return jax.shard_map(
        body,
        mesh=mesh,
        in_specs=placed,
        out_specs=(
            P(("dp", "expert"), None),
            P(("dp", "expert"), None, None),
            P(),
            P("expert", None, "dp"),
            P("expert", "dp", None),
        ),
        check_vma=False,
    )
```
